128 devices in a mesh: group: 8 (over x, core), member: 16 (over y, z).
Axes of the slice: x: 4, y: 4, z: 4, core: 2. Of those that a mesh axis runs over, the one named last changes fastest.
Arguments:
- pressure_init: float32 [262144], P(('group', 'member')), may hold values from 0.2 to 2
- gap_height: float32 [262144], P(('group', 'member'))
- active: int32 [262144], P(('group', 'member')), may hold values 0 or 1
- self_compliance: float32 [262144], P(('group', 'member')), may hold values from 1 to 3
- near_blocks: bfloat16 [1024, 9, 256, 256], P(('group', 'member')), may hold values from -0.059814453 to 0.059814453
- near_list: int32 [1024, 9], P(('group', 'member')), may hold values from 0 to 1023, as said below
- far_list: int32 [1024, 27], P(('group', 'member')), may hold values from 0 to 1023, as said below
- source_basis: bfloat16 [1024, 32, 256], P(('group', 'member')), may hold values from -0.375 to 0.375
- target_basis: bfloat16 [1024, 32, 256], P(('group', 'member')), may hold values from -0.3984375 to 0.3984375
- coupling: bfloat16 [1024, 27, 1024], P(('group', 'member')), may hold values from -0.21875 to 0.21875
Outputs:
- pressure: float32 [262144], P(('group', 'member'))
- gap: float32 [262144], P(('group', 'member'))
The draws below stay inside these ranges and needn't reach their ends.
Inputs may be any that keep to these rules, and one draw needn't show every extreme that they name: `near_list`: slot 0 of each row is the cluster itself; the other slots name distinct clusters whose index // 128 differs from the row's own by at most one. `far_list`: each row names distinct clusters, none of them in the same row of near_list.
All inputs are finite; a program needn't handle non-finite values. No bound on the sum of `active` on one device may be relied on, other than what follows from the above.
Results may differ from the reference program's by a relative error of at most 0.0035.
Values may be sent and summed in bfloat16 or wider, within the bound.
A program may use at most 64 MiB of HBM per device.

```python
import math
import jax
import jax.numpy as jnp
from jax import lax

CS = 256
R = 32
NEAR = 9
FAR = 27
ITERS = 2
CL_DEV = 8
CG = 128
ELEMENTS = 262144
CLUSTERS = 1024


def draw_lists(key):
    cluster_ids = jnp.arange(CLUSTERS, dtype=jnp.int32)
    group_of = cluster_ids // CG
    first_key, second_key = jax.random.split(key)
    near_scores = jax.random.randint(first_key, (CLUSTERS, CLUSTERS), 0, 1 << 19, dtype=jnp.int32) * CLUSTERS + cluster_ids[None, :]
    in_reach = jnp.abs(group_of[:, None] - group_of[None, :]) <= 1
    itself = cluster_ids[:, None] == cluster_ids[None, :]
    near_scores = jnp.where(in_reach & jnp.logical_not(itself), near_scores, -1)
    others = lax.top_k(near_scores, NEAR - 1)[1].astype(jnp.int32)
    near_list = jnp.concatenate([cluster_ids[:, None], others], axis=1)
    listed = jnp.any(near_list[:, :, None] == cluster_ids[None, None, :], axis=1)
    far_scores = jax.random.randint(second_key, (CLUSTERS, CLUSTERS), 0, 1 << 19, dtype=jnp.int32) * CLUSTERS + cluster_ids[None, :]
    far_scores = jnp.where(listed, -1, far_scores)
    far_list = lax.top_k(far_scores, FAR)[1].astype(jnp.int32)
    return (near_list, far_list)


def draw_near_list(key, part):
    lists = draw_lists(key)
    return lists[0]


def draw_far_list(key, part):
    lists = draw_lists(key)
    return lists[1]


def draw_gap_height(key, part):
    key = jax.random.fold_in(key, 5)
    position = jnp.arange(ELEMENTS, dtype=jnp.float32) / ELEMENTS
    ramp_scale = 1.0 + 2.0 * position
    values = jax.random.normal(key, (ELEMENTS,), jnp.float32) * ramp_scale
    return values.astype(jnp.float32)


def set_ends(drawn, rng, least, top_value):
    longest = drawn.shape.index(max(drawn.shape))
    spots = []
    for shift in (0, 1):
        where = [jax.random.randint(jax.random.fold_in(rng, axis), (), 0, length) for axis, length in enumerate(drawn.shape)]
        where[longest] = (where[longest] + shift) % drawn.shape[longest]
        spots.append(tuple(where))
    return drawn.at[spots[0]].set(least).at[spots[1]].set(top_value)


def block_levels(stream_key, extent, cuts, least, top_value):
    def one(axis_at, shards_of):
        heights = jax.random.uniform(jax.random.fold_in(jax.random.fold_in(stream_key, 6), axis_at), (shards_of,), jnp.float32, least / len(cuts), top_value / len(cuts))
        return jnp.repeat(jnp.exp(heights), extent[axis_at] // shards_of).reshape((-1,) + (1,) * (len(extent) - axis_at - 1))

    factor_of = one(*cuts[0])
    for cut in cuts[1:]:
        factor_of = factor_of * one(*cut)
    return factor_of


def gaussian(own_key, dims, width, most, cuts=(), kind=jnp.bfloat16):
    loudness = block_levels(own_key, dims, cuts, -0.22, 0.18) if cuts else 1.0
    array = jax.random.normal(own_key, dims, jnp.float32) * width * loudness
    return jnp.minimum(jnp.maximum(array, -most), most).astype(kind)


def setup_inputs(seed: int = 0) -> dict:
    keys = jax.random.split(jax.random.key(seed), 11)
    pressure_init = jnp.clip(jnp.exp(math.log(2.0) - 2.3025851 * jax.random.uniform(keys[0], (ELEMENTS,), jnp.float32) ** block_levels(keys[0], (ELEMENTS,), ((0, 128),), -0.2, 0.2)), 0.2, 2.0)
    gap_height = draw_gap_height(jax.random.fold_in(keys[10], 71), 0)
    active = set_ends((jax.random.randint(keys[2], (ELEMENTS,), 0, 4) < 3).astype(jnp.int32), jax.random.fold_in(keys[2], 1), 0, 1)
    self_compliance = jnp.clip(jnp.exp(math.log(3.0) - 1.0986123 * jax.random.uniform(keys[3], (ELEMENTS,), jnp.float32) ** block_levels(keys[3], (ELEMENTS,), ((0, 128),), -0.2, 0.2)), 1.0, 3.0)
    near_blocks = gaussian(keys[4], (CLUSTERS, NEAR, CS, CS), 0.01, 0.059814453, ((0, 128),))
    near_list = draw_near_list(jax.random.fold_in(keys[10], 71), 0)
    far_list = draw_far_list(jax.random.fold_in(keys[10], 71), 0)
    source_basis = gaussian(keys[7], (CLUSTERS, R, CS), CS ** -0.5, 0.375, ((0, 128),))
    target_basis = gaussian(keys[8], (CLUSTERS, R, CS), 0.07, 0.3984375, ((0, 128),))
    coupling = gaussian(keys[9], (CLUSTERS, FAR, R * R), (FAR * R) ** -0.5, 0.21875, ((0, 128),))
    return {"pressure_init": pressure_init, "gap_height": gap_height, "active": active, "self_compliance": self_compliance, "near_blocks": near_blocks, "near_list": near_list, "far_list": far_list, "source_basis": source_basis, "target_basis": target_basis, "coupling": coupling}


def near_product(pieces):
    return jnp.einsum("cnij,cnj->ci", pieces[0].astype(jnp.float32), pieces[1].astype(jnp.float32))


def operate(direction, self_compliance, near_blocks, near_list, far_list, source_basis, target_basis, coupling):
    narrow = direction.astype(jnp.bfloat16)
    local_rows = narrow.reshape(CLUSTERS, CS)
    near_rows = local_rows[near_list]
    blocks_count = CLUSTERS // CL_DEV
    near_part = lax.map(near_product, (near_blocks.reshape(blocks_count, CL_DEV, NEAR, CS, CS), near_rows.reshape(blocks_count, CL_DEV, NEAR, CS)))
    near_part = near_part.reshape(CLUSTERS, CS)
    projected = jnp.einsum("cai,ci->ca", source_basis.astype(jnp.float32), local_rows.astype(jnp.float32)).astype(jnp.bfloat16)
    picked = projected[far_list]
    coupled = jnp.einsum("cfab,cfb->ca", coupling.reshape(CLUSTERS, FAR, R, R).astype(jnp.float32), picked.astype(jnp.float32)).astype(jnp.bfloat16)
    far_part = jnp.einsum("cai,ca->ci", target_basis.astype(jnp.float32), coupled.astype(jnp.float32))
    return self_compliance * narrow.astype(jnp.float32) + (near_part + far_part).reshape(ELEMENTS)


def reference(pressure_init, gap_height, active, self_compliance, near_blocks, near_list, far_list, source_basis, target_basis, coupling):
    weight = active.astype(jnp.float32)
    active_total = jnp.sum(weight)

    def apply_h(field):
        return operate(field, self_compliance, near_blocks, near_list, far_list, source_basis, target_basis, coupling)

    pressure = pressure_init * weight
    gap = apply_h(pressure) - gap_height
    direction = jnp.zeros_like(gap)
    norm_old = jnp.float32(1.0)
    for iteration in range(ITERS):
        gap_mean = jnp.sum(weight * gap) / active_total
        shifted = (gap - gap_mean) * weight
        norm_now = jnp.sum(shifted * shifted)
        if iteration == 0:
            direction = shifted
        else:
            direction = shifted + (norm_now / norm_old) * direction
        image = apply_h(direction)
        image_mean = jnp.sum(weight * image) / active_total
        descent = jnp.sum(shifted * direction)
        curvature = jnp.sum((image - image_mean) * weight * direction)
        step_length = descent / curvature
        pressure = pressure - step_length * direction
        gap = gap - step_length * image
        norm_old = norm_now
    return pressure, gap
```

```python
import functools

import jax
import jax.numpy as jnp
from jax import lax
from jax.experimental import pallas as pl
from jax.experimental.pallas import tpu as pltpu
from jax.sharding import PartitionSpec as P

MESH = pl.DeviceIdType.MESH
F32 = jnp.float32
BF16 = jnp.bfloat16
GROUPS = 8
MEMBERS = 16
DEVICES = GROUPS * MEMBERS
CL = 8
CS = 256
RANK = 32
NEAR = 9
FAR = 27
WINDOW = 3 * MEMBERS
SCALE = 2.0**-20


def dot(a, b, dims=((1,), (0,))):
    return lax.dot_general(a, b, (dims, ((), ())), preferred_element_type=F32)


def split3(a):
    hi = a.astype(BF16)
    rest = a - hi.astype(F32)
    mid = rest.astype(BF16)
    low = (rest - mid.astype(F32)).astype(BF16)
    return hi, mid, low


def total(a):
    return jnp.sum(jnp.sum(a, axis=0, keepdims=True), axis=1, keepdims=True)


def kernel(
    pressure_hbm,
    height_hbm,
    active_hbm,
    self_hbm,
    near_hbm,
    near_list_hbm,
    far_list_hbm,
    source_hbm,
    target_hbm,
    coupling_hbm,
    pressure_out,
    gap_out,
    pressure_v,
    height_v,
    active_v,
    self_v,
    near_v,
    near_list_v,
    far_list_v,
    source_v,
    target_v,
    coupling_v,
    far_pad,
    near_pick,
    near_dev,
    far_pick,
    far_seg,
    spread,
    fold,
    rows_v,
    couple_v,
    field_out,
    field_in,
    proj0_out,
    proj0_in,
    proj_out,
    proj_in,
    last_out,
    last_in,
    load_sem,
    field_send,
    field_recv,
    proj_send,
    proj_recv,
):
    g = lax.axis_index("group")
    m = lax.axis_index("member")

    def peer(slot):
        return (
            lax.rem(g + lax.div(slot, MEMBERS), GROUPS),
            lax.rem(m + lax.rem(slot, MEMBERS), MEMBERS),
        )

    barrier = pltpu.get_barrier_semaphore()

    def greet(slot, carry):
        pl.semaphore_signal(barrier, inc=1, device_id=peer(slot), device_id_type=MESH)
        return carry

    lax.fori_loop(1, DEVICES, greet, 0)

    pairs = (
        (pressure_hbm, pressure_v),
        (active_hbm, active_v),
        (source_hbm, source_v),
        (near_list_hbm, near_list_v),
        (far_list_hbm, far_list_v),
        (self_hbm, self_v),
        (height_hbm, height_v),
        (coupling_hbm, coupling_v),
        (target_hbm, target_v),
        (near_hbm, near_v),
    )
    loads = [pltpu.make_async_copy(a, b, load_sem.at[i]) for i, (a, b) in enumerate(pairs)]
    for load in loads:
        load.start()

    def wide(ref):
        return jnp.concatenate(
            [ref[pl.ds(0, CL, stride=2), :], ref[pl.ds(1, CL, stride=2), :]], axis=1
        )

    def tall(value):
        return jnp.concatenate([value[:, :128], value[:, 128:]], axis=0)

    row8 = lax.broadcasted_iota(jnp.int32, (CL, CS), 0)
    lane8 = lax.broadcasted_iota(jnp.int32, (CL, CS), 1)
    own = row8 == lax.shift_right_logical(lane8, 5)

    def project(value16):
        product = dot(value16, source_v[...], ((1,), (1,)))
        first = jnp.sum(jnp.where(own, product[:CL], 0.0), axis=0, keepdims=True)
        second = jnp.sum(jnp.where(own, product[CL:], 0.0), axis=0, keepdims=True)
        return first, second

    lane1 = lax.broadcasted_iota(jnp.int32, (1, 128), 1)

    def scalar_row(*values):
        row = jnp.zeros((1, 128), F32)
        for i, value in enumerate(values):
            row = jnp.where(lane1 == i, value, row)
        return row

    def field_copy(phase, slot):
        far_slot = jnp.where(slot >= 2 * MEMBERS, slot + (GROUPS - 3) * MEMBERS, slot)
        return pltpu.make_async_remote_copy(
            src_ref=field_out.at[phase],
            dst_ref=field_in.at[phase, slot],
            send_sem=field_send.at[phase],
            recv_sem=field_recv.at[phase],
            device_id=peer(far_slot),
            device_id_type=MESH,
        )

    def field_all(phase):
        rest = field_in.at[phase, pl.ds(1, WINDOW - 1)]
        return pltpu.make_async_remote_copy(
            src_ref=rest,
            dst_ref=rest,
            send_sem=field_send.at[phase],
            recv_sem=field_recv.at[phase],
            device_id=peer(1),
            device_id_type=MESH,
        )

    def proj_copy(out, into, sem, slot):
        return pltpu.make_async_remote_copy(
            src_ref=out,
            dst_ref=into.at[slot],
            send_sem=proj_send.at[sem],
            recv_sem=proj_recv.at[sem],
            device_id=peer(slot),
            device_id_type=MESH,
        )

    def proj_all(into, sem):
        rest = into.at[pl.ds(1, DEVICES - 1)]
        return pltpu.make_async_remote_copy(
            src_ref=rest,
            dst_ref=rest,
            send_sem=proj_send.at[sem],
            recv_sem=proj_recv.at[sem],
            device_id=peer(1),
            device_id_type=MESH,
        )

    def send_field(phase, value):
        block = tall(value).astype(BF16)
        field_out[phase] = block
        field_in[phase, 0] = block

        def one(slot, carry):
            field_copy(phase, slot).start()
            return carry

        lax.fori_loop(1, WINDOW, one, 0)

    def send_proj(out, into, sem, rows):
        for i, row in enumerate(rows):
            out[i : i + 1, :] = row
            into[0, i : i + 1, :] = row

        def one(slot, carry):
            proj_copy(out, into, sem, slot).start()
            return carry

        lax.fori_loop(1, DEVICES, one, 0)

    loads[0].wait()
    loads[1].wait()
    mask = wide(active_v).astype(F32)
    pressure = wide(pressure_v) * mask
    loads[2].wait()
    first, mask_proj = project(jnp.concatenate([pressure, mask], axis=0).astype(BF16))
    count_own = total(mask)

    pl.semaphore_wait(barrier, DEVICES - 1)
    send_field(0, pressure)
    send_proj(proj0_out, proj0_in, 0, (first[:, :128], first[:, 128:]))
    send_proj(
        proj_out.at[0],
        proj_in.at[0],
        1,
        (mask_proj[:, :128], mask_proj[:, 128:], scalar_row(count_own)),
    )

    loads[3].wait()
    loads[4].wait()
    far_pad[...] = jnp.zeros_like(far_pad)
    far_pad[:, :FAR] = far_list_v[...].astype(F32)
    far_cols = jnp.transpose(far_pad[...])
    near_ids = near_list_v[...]
    dg = lax.bitwise_and(g - lax.shift_right_logical(near_ids, 7), 7)
    dm = lax.bitwise_and(m - lax.bitwise_and(lax.shift_right_logical(near_ids, 3), 15), 15)
    near_slot = jnp.where(dg == 7, 2, dg) * MEMBERS + dm
    near_row = near_slot * (2 * CL) + lax.bitwise_and(near_ids, 7)
    dev_row = dg * MEMBERS + dm
    pick_iota = lax.broadcasted_iota(jnp.int32, (CL, WINDOW * 2 * CL), 1)
    dev_iota = lax.broadcasted_iota(jnp.int32, (CL, DEVICES), 1)
    low, high, dev = [], [], []
    for n in range(NEAR):
        low.append(jnp.where(pick_iota == near_row[:, n : n + 1], 1.0, 0.0))
        high.append(jnp.where(pick_iota == near_row[:, n : n + 1] + CL, 1.0, 0.0))
        dev.append(jnp.where(dev_iota == dev_row[:, n : n + 1], 1.0, 0.0))
    near_pick[...] = jnp.concatenate(low + high, axis=0).astype(BF16)
    near_dev[...] = jnp.concatenate(dev, axis=0).astype(BF16)

    far_ids = far_cols[:RANK, :].astype(jnp.int32)
    fg = lax.bitwise_and(g - lax.shift_right_logical(far_ids, 7), 7)
    fm = lax.bitwise_and(m - lax.bitwise_and(lax.shift_right_logical(far_ids, 3), 15), 15)
    there = lax.broadcasted_iota(jnp.int32, (RANK, CL), 0) < FAR
    far_row = jnp.where(there, fg * MEMBERS + fm, -1)
    far_part = lax.bitwise_and(far_ids, 7)
    far_iota = lax.broadcasted_iota(jnp.int32, (RANK, DEVICES), 1)
    part_iota = lax.shift_right_logical(lax.broadcasted_iota(jnp.int32, (RANK, CS), 1), 5)
    for c in range(CL):
        rows = pl.ds(c * RANK, RANK)
        far_pick[rows, :] = jnp.where(far_iota == far_row[:, c : c + 1], 1.0, 0.0).astype(BF16)
        far_seg[rows, :] = jnp.where(part_iota == far_part[:, c : c + 1], 1.0, 0.0)
    tall_iota = lax.bitwise_and(lax.broadcasted_iota(jnp.int32, (CS, RANK * RANK), 0), RANK - 1)
    wide_iota = lax.bitwise_and(lax.broadcasted_iota(jnp.int32, (CS, RANK * RANK), 1), RANK - 1)
    spread[...] = jnp.where(tall_iota == wide_iota, 1.0, 0.0).astype(BF16)
    tall_iota = lax.shift_right_logical(lax.broadcasted_iota(jnp.int32, (RANK * RANK, CS), 0), 5)
    wide_iota = lax.bitwise_and(lax.broadcasted_iota(jnp.int32, (RANK * RANK, CS), 1), RANK - 1)
    fold[...] = jnp.where(tall_iota == wide_iota, 1.0, 0.0).astype(BF16)
    for load in loads[5:]:
        load.wait()
    compliance = wide(self_v)
    height = wide(height_v)

    row16 = lax.broadcasted_iota(jnp.int32, (2 * CL, CS), 0)

    def gather_field(phase):
        window = field_in[phase].reshape(WINDOW * 2 * CL, 128)
        picked = dot(near_pick[...], window)
        half = NEAR * CL
        return jnp.concatenate([picked[:half], picked[half:]], axis=1)

    def near_sum(rows):
        rows_v[...] = rows

        def cluster(c, acc):
            for n in range(NEAR):
                row = rows_v[pl.ds(n * CL + c, 1), :]
                left = jnp.where(row16 == c, row, 0.0).astype(BF16)
                acc = acc + dot(left, near_v[c, n], ((1,), (1,)))
            return acc

        return lax.fori_loop(0, CL, cluster, jnp.zeros((2 * CL, CS), F32))[:CL]

    def far_sum(projected):
        picked = dot(far_pick[...], projected.astype(BF16))
        spreaded = dot((picked * far_seg[...]).astype(BF16), spread[...])
        for c in range(CL):
            part = spreaded[c * RANK : c * RANK + FAR] * coupling_v[c].astype(F32)
            couple_v[c : c + 1, :] = jnp.sum(part, axis=0, keepdims=True)
        hi, mid, low = split3(couple_v[...])
        coupled = dot(hi, fold[...]) + (dot(mid, fold[...]) + dot(low, fold[...]))
        return dot(jnp.where(own, coupled, 0.0).astype(BF16), target_v[...])

    def operate(value, rows, projected):
        narrow = value.astype(BF16).astype(F32)
        return compliance * narrow + (near_sum(rows) + far_sum(projected))

    def proj_rows(ref):
        return jnp.concatenate([ref[:, 0, :], ref[:, 1, :]], axis=1)

    def near_scalars(scalars):
        hi, mid, low = split3(scalars)
        return dot(near_dev[...], hi) + (dot(near_dev[...], mid) + dot(near_dev[...], low))

    field_all(0).wait_recv()
    proj_all(proj0_in, 0).wait_recv()
    rows0 = gather_field(0)
    mask_rows = jnp.where(rows0 != 0.0, 1.0, 0.0)
    gap = operate(pressure, rows0, proj_rows(proj0_in)) - height

    safe_count = jnp.maximum(count_own, 1.0)
    gap_sum = total(mask * gap)
    gap_centre = gap_sum / safe_count
    local = (gap - gap_centre) * mask
    send_field(1, local)
    zeros = jnp.zeros_like(local)
    first, _ = project(jnp.concatenate([local, zeros], axis=0).astype(BF16))
    send_proj(
        proj_out.at[1],
        proj_in.at[1],
        2,
        (first[:, :128], first[:, 128:], scalar_row(gap_sum, gap_centre)),
    )

    proj_all(proj_in.at[0], 1).wait_recv()
    mask_projs = proj_rows(proj_in.at[0])
    counts = proj_in[0, :, 2, :][:, 0:1]
    count = jnp.sum(counts, axis=0, keepdims=True)

    field_all(1).wait_recv()
    proj_all(proj_in.at[1], 2).wait_recv()
    scalars = proj_in[1, :, 2, :]
    gap_mean = jnp.sum(scalars[:, 0:1], axis=0, keepdims=True) / count
    direction = (gap - gap_mean) * mask
    here = near_scalars(scalars)
    rows1 = gather_field(1) + (here[:, 1:2] - gap_mean) * mask_rows
    projs1 = proj_rows(proj_in.at[1]) + (scalars[:, 1:2] - gap_mean) * mask_projs
    image = operate(direction, rows1, projs1)

    image_sum = total(mask * image)
    image_centre = image_sum / safe_count
    centred = (image - image_centre) * mask
    norm_own = total(direction * direction)
    fit = total(centred * direction) / jnp.where(norm_own > 0.0, norm_own, 1.0)
    local = centred - fit * direction
    send_field(2, local)
    first, _ = project(jnp.concatenate([local, zeros], axis=0).astype(BF16))
    small = centred * SCALE
    send_proj(
        proj_out.at[2],
        proj_in.at[2],
        3,
        (
            first[:, :128],
            first[:, 128:],
            scalar_row(
                image_sum,
                total(mask * image * direction),
                total(mask * direction),
                norm_own,
                total(small * small),
                image_centre,
                fit,
            ),
        ),
    )

    field_all(2).wait_recv()
    proj_all(proj_in.at[2], 3).wait_recv()
    scalars = proj_in[2, :, 2, :]
    sums = jnp.sum(scalars, axis=0, keepdims=True)
    image_mean = sums[:, 0:1] / count
    norm_old = sums[:, 3:4]
    step = norm_old / (sums[:, 1:2] - image_mean * sums[:, 2:3])
    shifts = scalars[:, 5:6] - image_mean
    small_shifts = shifts * SCALE
    spread_sum = sums[:, 4:5] + jnp.sum(
        counts * (small_shifts * small_shifts), axis=0, keepdims=True
    )
    long_step = step / SCALE
    norm_now = long_step * (long_step * spread_sum) - norm_old
    ratio = norm_now / norm_old
    pressure = pressure - step * direction
    gap = gap - step * image
    shifted = (gap - (gap_mean - step * image_mean)) * mask
    previous = direction
    direction = shifted + ratio * previous
    here = near_scalars(scalars)
    rows2 = (
        (1.0 + ratio - step * here[:, 6:7]) * rows1
        - step * gather_field(2)
        - step * (here[:, 5:6] - image_mean) * mask_rows
    )
    projs2 = (
        (1.0 + ratio - step * scalars[:, 6:7]) * projs1
        - step * proj_rows(proj_in.at[2])
        - step * shifts * mask_projs
    )
    image = operate(direction, rows2, projs2)

    send_proj(
        last_out,
        last_in,
        4,
        (
            scalar_row(
                total(mask * image),
                total(mask * image * direction),
                total(mask * direction),
                total(shifted * direction),
            ),
        ),
    )
    proj_all(last_in, 4).wait_recv()
    sums = jnp.sum(last_in[:, 0, :], axis=0, keepdims=True)
    image_mean = sums[:, 0:1] / count
    step = sums[:, 3:4] / (sums[:, 1:2] - image_mean * sums[:, 2:3])
    pressure = pressure - step * direction
    gap = gap - step * image
    for ref, value in ((pressure_out, pressure), (gap_out, gap)):
        ref[pl.ds(0, CL, stride=2), :] = value[:, :128]
        ref[pl.ds(1, CL, stride=2), :] = value[:, 128:]

    for phase in range(3):
        field_all(phase).wait_send()
    proj_all(proj0_in, 0).wait_send()
    for i in range(3):
        proj_all(proj_in.at[i], i + 1).wait_send()
    proj_all(last_in, 4).wait_send()


def shards(
    pressure_init,
    gap_height,
    active,
    self_compliance,
    near_blocks,
    near_list,
    far_list,
    source_basis,
    target_basis,
    coupling,
):
    elements = pressure_init.shape[0]
    fold_shape = (elements // 128, 128)
    vmem = pltpu.VMEM
    scratch = [
        vmem(fold_shape, F32),
        vmem(fold_shape, F32),
        vmem(fold_shape, jnp.int32),
        vmem(fold_shape, F32),
        vmem((CL, NEAR, CS, CS), BF16),
        vmem((CL, NEAR), jnp.int32),
        vmem((CL, FAR), jnp.int32),
        vmem((CL * RANK, CS), BF16),
        vmem((CL * RANK, CS), BF16),
        vmem((CL, FAR, RANK * RANK), BF16),
        vmem((CL, 128), F32),
        vmem((2 * NEAR * CL, WINDOW * 2 * CL), BF16),
        vmem((NEAR * CL, DEVICES), BF16),
        vmem((CL * RANK, DEVICES), BF16),
        vmem((CL * RANK, CS), F32),
        vmem((CS, RANK * RANK), BF16),
        vmem((RANK * RANK, CS), BF16),
        vmem((NEAR * CL, CS), F32),
        vmem((CL, RANK * RANK), F32),
        vmem((3, 2 * CL, 128), BF16),
        vmem((3, WINDOW, 2 * CL, 128), BF16),
        vmem((2, 128), F32),
        vmem((DEVICES, 2, 128), F32),
        vmem((3, 3, 128), F32),
        vmem((3, DEVICES, 3, 128), F32),
        vmem((1, 128), F32),
        vmem((DEVICES, 1, 128), F32),
        pltpu.SemaphoreType.DMA((10,)),
        pltpu.SemaphoreType.DMA((3,)),
        pltpu.SemaphoreType.DMA((3,)),
        pltpu.SemaphoreType.DMA((5,)),
        pltpu.SemaphoreType.DMA((5,)),
    ]
    pressure, gap = pl.pallas_call(
        kernel,
        out_shape=[jax.ShapeDtypeStruct(fold_shape, F32)] * 2,
        in_specs=[pl.BlockSpec(memory_space=pl.ANY)] * 10,
        out_specs=[pl.BlockSpec(memory_space=pltpu.VMEM)] * 2,
        scratch_shapes=scratch,
        compiler_params=pltpu.CompilerParams(
            collective_id=0, has_side_effects=True, vmem_limit_bytes=40 * 2**20
        ),
    )(
        pressure_init.reshape(fold_shape),
        gap_height.reshape(fold_shape),
        active.reshape(fold_shape),
        self_compliance.reshape(fold_shape),
        near_blocks,
        near_list,
        far_list,
        source_basis.reshape(CL * RANK, CS),
        target_basis.reshape(CL * RANK, CS),
        coupling,
    )
    return pressure.reshape(elements), gap.reshape(elements)


def solution(mesh):
    spec = P(("group", "member"))
    return jax.shard_map(
        shards, mesh=mesh, in_specs=(spec,) * 10, out_specs=(spec, spec), check_vma=False
    )
```

```python
import functools

import jax
import jax.numpy as jnp
from jax import lax
from jax.experimental import pallas as pl
from jax.experimental.pallas import tpu as pltpu
from jax.sharding import PartitionSpec as P

MESH = pl.DeviceIdType.MESH
F32 = jnp.float32
BF16 = jnp.bfloat16
GROUPS = 8
MEMBERS = 16
DEVICES = GROUPS * MEMBERS
CL = 8
CS = 256
RANK = 32
NEAR = 9
FAR = 27
WINDOW = 3 * MEMBERS
SCALE = 2.0**-20


def hops(slot):
    steps = (slot & 3, slot >> 2 & 3, slot >> 5)
    return sum(min(step, 4 - step) for step in steps)


FAR_FIRST = sorted(range(1, DEVICES), key=lambda slot: -hops(slot))
FIELD_FIRST = sorted(range(1, WINDOW), key=lambda slot: -hops(slot % MEMBERS))


def dot(a, b, dims=((1,), (0,))):
    return lax.dot_general(a, b, (dims, ((), ())), preferred_element_type=F32)


def split3(a):
    hi = a.astype(BF16)
    rest = a - hi.astype(F32)
    mid = rest.astype(BF16)
    low = (rest - mid.astype(F32)).astype(BF16)
    return hi, mid, low


def total(a):
    return jnp.sum(jnp.sum(a, axis=0, keepdims=True), axis=1, keepdims=True)


def kernel(
    pressure_hbm,
    height_hbm,
    active_hbm,
    self_hbm,
    near_hbm,
    near_list_hbm,
    far_list_hbm,
    source_hbm,
    target_hbm,
    coupling_hbm,
    pressure_out,
    gap_out,
    pressure_v,
    height_v,
    active_v,
    self_v,
    near_v,
    near_list_v,
    far_list_v,
    source_v,
    target_v,
    coupling_v,
    far_pad,
    near_pick,
    near_dev,
    far_pick,
    far_seg,
    spread,
    fold,
    rows_v,
    couple_v,
    field_out,
    field_in,
    proj0_out,
    proj0_in,
    proj_out,
    proj_in,
    last_out,
    last_in,
    load_sem,
    field_send,
    field_recv,
    proj_send,
    proj_recv,
):
    g = lax.axis_index("group")
    m = lax.axis_index("member")

    def around(dy, dz):
        return lax.bitwise_and(m + 4 * dy, 12) + lax.bitwise_and(m + dz, 3)

    groups = [lax.bitwise_and(g + 2 * dx, 6) + lax.bitwise_xor(lax.bitwise_and(g, 1), dc) for dx in range(4) for dc in range(2)]
    members = [around(dy, dz) for dy in range(4) for dz in range(4)]
    sides = (g, lax.bitwise_and(g + 1, 7), lax.bitwise_and(g + 7, 7))

    def peer(slot):
        return groups[slot // MEMBERS], members[slot % MEMBERS]

    barrier = pltpu.get_barrier_semaphore()

    for slot in FAR_FIRST:
        pl.semaphore_signal(barrier, inc=1, device_id=peer(slot), device_id_type=MESH)

    pairs = (
        (pressure_hbm, pressure_v),
        (active_hbm, active_v),
        (source_hbm, source_v),
        (near_list_hbm, near_list_v),
        (far_list_hbm, far_list_v),
        (self_hbm, self_v),
        (height_hbm, height_v),
        (coupling_hbm, coupling_v),
        (target_hbm, target_v),
        (near_hbm, near_v),
    )
    loads = [pltpu.make_async_copy(a, b, load_sem.at[i]) for i, (a, b) in enumerate(pairs)]
    for load in loads:
        load.start()

    def wide(ref):
        return jnp.concatenate(
            [ref[pl.ds(0, CL, stride=2), :], ref[pl.ds(1, CL, stride=2), :]], axis=1
        )

    def tall(value):
        return jnp.concatenate([value[:, :128], value[:, 128:]], axis=0)

    row8 = lax.broadcasted_iota(jnp.int32, (CL, CS), 0)
    lane8 = lax.broadcasted_iota(jnp.int32, (CL, CS), 1)
    own = row8 == lax.shift_right_logical(lane8, 5)

    def project(value16):
        product = dot(value16, source_v[...], ((1,), (1,)))
        first = jnp.sum(jnp.where(own, product[:CL], 0.0), axis=0, keepdims=True)
        second = jnp.sum(jnp.where(own, product[CL:], 0.0), axis=0, keepdims=True)
        return first, second

    lane1 = lax.broadcasted_iota(jnp.int32, (1, 128), 1)

    def scalar_row(*values):
        row = jnp.zeros((1, 128), F32)
        for i, value in enumerate(values):
            row = jnp.where(lane1 == i, value, row)
        return row

    def field_copy(phase, slot):
        return pltpu.make_async_remote_copy(
            src_ref=field_out.at[phase],
            dst_ref=field_in.at[phase, slot],
            send_sem=field_send.at[phase],
            recv_sem=field_recv.at[phase],
            device_id=(sides[slot // MEMBERS], members[slot % MEMBERS]),
            device_id_type=MESH,
        )

    def field_all(phase):
        rest = field_in.at[phase, pl.ds(1, WINDOW - 1)]
        return pltpu.make_async_remote_copy(
            src_ref=rest,
            dst_ref=rest,
            send_sem=field_send.at[phase],
            recv_sem=field_recv.at[phase],
            device_id=peer(1),
            device_id_type=MESH,
        )

    def proj_copy(out, into, sem, slot):
        return pltpu.make_async_remote_copy(
            src_ref=out,
            dst_ref=into.at[slot],
            send_sem=proj_send.at[sem],
            recv_sem=proj_recv.at[sem],
            device_id=peer(slot),
            device_id_type=MESH,
        )

    def proj_all(into, sem):
        rest = into.at[pl.ds(1, DEVICES - 1)]
        return pltpu.make_async_remote_copy(
            src_ref=rest,
            dst_ref=rest,
            send_sem=proj_send.at[sem],
            recv_sem=proj_recv.at[sem],
            device_id=peer(1),
            device_id_type=MESH,
        )

    def send_field(phase, value):
        block = tall(value).astype(BF16)
        field_out[phase] = block
        field_in[phase, 0] = block
        for slot in FIELD_FIRST:
            field_copy(phase, slot).start()

    def send_proj(out, into, sem, rows):
        for i, row in enumerate(rows):
            out[i : i + 1, :] = row
            into[0, i : i + 1, :] = row
        for slot in FAR_FIRST:
            proj_copy(out, into, sem, slot).start()

    loads[0].wait()
    loads[1].wait()
    mask = wide(active_v).astype(F32)
    pressure = wide(pressure_v) * mask
    loads[2].wait()
    first, mask_proj = project(jnp.concatenate([pressure, mask], axis=0).astype(BF16))
    count_own = total(mask)

    loads[3].wait()
    loads[4].wait()
    far_pad[...] = jnp.zeros_like(far_pad)
    far_pad[:, :FAR] = far_list_v[...].astype(F32)
    far_cols = jnp.transpose(far_pad[...])
    near_ids = near_list_v[...]

    def member_part(ids):
        dy = lax.bitwise_and(m - lax.bitwise_and(lax.shift_right_logical(ids, 3), 12), 12)
        return dy + lax.bitwise_and(m - lax.shift_right_logical(ids, 3), 3)

    def group_part(ids):
        theirs = lax.shift_right_logical(ids, 7)
        dx = lax.bitwise_and(g - lax.bitwise_and(theirs, 6), 6)
        return (dx + lax.bitwise_and(g + theirs, 1)) * MEMBERS

    dg = lax.bitwise_and(g - lax.shift_right_logical(near_ids, 7), 7)
    near_slot = jnp.where(dg == 7, 2, dg) * MEMBERS + member_part(near_ids)
    near_row = near_slot * (2 * CL) + lax.bitwise_and(near_ids, 7)
    dev_row = group_part(near_ids) + member_part(near_ids)
    pick_iota = lax.broadcasted_iota(jnp.int32, (CL, WINDOW * 2 * CL), 1)
    dev_iota = lax.broadcasted_iota(jnp.int32, (CL, DEVICES), 1)
    low, high, dev = [], [], []
    for n in range(NEAR):
        low.append(jnp.where(pick_iota == near_row[:, n : n + 1], 1.0, 0.0))
        high.append(jnp.where(pick_iota == near_row[:, n : n + 1] + CL, 1.0, 0.0))
        dev.append(jnp.where(dev_iota == dev_row[:, n : n + 1], 1.0, 0.0))
    near_pick[...] = jnp.concatenate(low + high, axis=0).astype(BF16)
    near_dev[...] = jnp.concatenate(dev, axis=0).astype(BF16)

    far_ids = far_cols[:RANK, :].astype(jnp.int32)
    there = lax.broadcasted_iota(jnp.int32, (RANK, CL), 0) < FAR
    far_row = jnp.where(there, group_part(far_ids) + member_part(far_ids), -1)
    far_part = lax.bitwise_and(far_ids, 7)
    far_iota = lax.broadcasted_iota(jnp.int32, (RANK, DEVICES), 1)
    part_iota = lax.shift_right_logical(lax.broadcasted_iota(jnp.int32, (RANK, CS), 1), 5)
    for c in range(CL):
        rows = pl.ds(c * RANK, RANK)
        far_pick[rows, :] = jnp.where(far_iota == far_row[:, c : c + 1], 1.0, 0.0).astype(BF16)
        far_seg[rows, :] = jnp.where(part_iota == far_part[:, c : c + 1], 1.0, 0.0)
    tall_iota = lax.bitwise_and(lax.broadcasted_iota(jnp.int32, (CS, RANK * RANK), 0), RANK - 1)
    wide_iota = lax.bitwise_and(lax.broadcasted_iota(jnp.int32, (CS, RANK * RANK), 1), RANK - 1)
    spread[...] = jnp.where(tall_iota == wide_iota, 1.0, 0.0).astype(BF16)
    tall_iota = lax.shift_right_logical(lax.broadcasted_iota(jnp.int32, (RANK * RANK, CS), 0), 5)
    wide_iota = lax.bitwise_and(lax.broadcasted_iota(jnp.int32, (RANK * RANK, CS), 1), RANK - 1)
    fold[...] = jnp.where(tall_iota == wide_iota, 1.0, 0.0).astype(BF16)
    pl.semaphore_wait(barrier, DEVICES - 1)
    send_field(0, pressure)
    send_proj(proj0_out, proj0_in, 0, (first[:, :128], first[:, 128:]))
    send_proj(
        proj_out.at[0],
        proj_in.at[0],
        1,
        (mask_proj[:, :128], mask_proj[:, 128:], scalar_row(count_own)),
    )

    for load in loads[5:]:
        load.wait()
    compliance = wide(self_v)
    height = wide(height_v)

    def turn(c, carry):
        for n in range(NEAR):
            near_v[c, n] = jnp.transpose(near_v[c, n])
        return carry

    lax.fori_loop(0, CL, turn, 0)

    row16 = lax.broadcasted_iota(jnp.int32, (2 * CL, CS), 0)

    def gather_field(phase):
        window = field_in[phase].reshape(WINDOW * 2 * CL, 128)
        picked = dot(near_pick[...], window)
        half = NEAR * CL
        return jnp.concatenate([picked[:half], picked[half:]], axis=1)

    def near_sum(rows):
        rows_v[...] = rows

        acc = jnp.zeros((2 * CL, CS), F32)
        for c in range(CL):
            for n in range(NEAR):
                row = rows_v[n * CL + c : n * CL + c + 1, :]
                left = jnp.where(row16 == c, row, 0.0).astype(BF16)
                acc = acc + dot(left, near_v[c, n])
        return acc[:CL]

    def far_sum(projected):
        picked = dot(far_pick[...], projected.astype(BF16))
        spreaded = dot((picked * far_seg[...]).astype(BF16), spread[...])
        for c in range(CL):
            part = spreaded[c * RANK : c * RANK + FAR] * coupling_v[c].astype(F32)
            couple_v[c : c + 1, :] = jnp.sum(part, axis=0, keepdims=True)
        hi, mid, low = split3(couple_v[...])
        coupled = dot(hi, fold[...]) + (dot(mid, fold[...]) + dot(low, fold[...]))
        return dot(jnp.where(own, coupled, 0.0).astype(BF16), target_v[...])

    def operate(value, rows, projected):
        narrow = value.astype(BF16).astype(F32)
        return compliance * narrow + (near_sum(rows) + far_sum(projected))

    def proj_rows(ref):
        return jnp.concatenate([ref[:, 0, :], ref[:, 1, :]], axis=1)

    def near_scalars(scalars):
        hi, mid, low = split3(scalars)
        return dot(near_dev[...], hi) + (dot(near_dev[...], mid) + dot(near_dev[...], low))

    field_all(0).wait_recv()
    proj_all(proj0_in, 0).wait_recv()
    rows0 = gather_field(0)
    mask_rows = jnp.where(rows0 != 0.0, 1.0, 0.0)
    gap = operate(pressure, rows0, proj_rows(proj0_in)) - height

    safe_count = jnp.maximum(count_own, 1.0)
    gap_sum = total(mask * gap)
    gap_centre = gap_sum / safe_count
    local = (gap - gap_centre) * mask
    send_field(1, local)
    zeros = jnp.zeros_like(local)
    first, _ = project(jnp.concatenate([local, zeros], axis=0).astype(BF16))
    send_proj(
        proj_out.at[1],
        proj_in.at[1],
        2,
        (first[:, :128], first[:, 128:], scalar_row(gap_sum, gap_centre)),
    )

    proj_all(proj_in.at[0], 1).wait_recv()
    mask_projs = proj_rows(proj_in.at[0])
    counts = proj_in[0, :, 2, :][:, 0:1]
    count = jnp.sum(counts, axis=0, keepdims=True)

    field_all(1).wait_recv()
    proj_all(proj_in.at[1], 2).wait_recv()
    scalars = proj_in[1, :, 2, :]
    gap_mean = jnp.sum(scalars[:, 0:1], axis=0, keepdims=True) / count
    direction = (gap - gap_mean) * mask
    here = near_scalars(scalars)
    rows1 = gather_field(1) + (here[:, 1:2] - gap_mean) * mask_rows
    projs1 = proj_rows(proj_in.at[1]) + (scalars[:, 1:2] - gap_mean) * mask_projs
    image = operate(direction, rows1, projs1)

    image_sum = total(mask * image)
    image_centre = image_sum / safe_count
    centred = (image - image_centre) * mask
    norm_own = total(direction * direction)
    fit = total(centred * direction) / jnp.where(norm_own > 0.0, norm_own, 1.0)
    local = centred - fit * direction
    send_field(2, local)
    first, _ = project(jnp.concatenate([local, zeros], axis=0).astype(BF16))
    small = centred * SCALE
    send_proj(
        proj_out.at[2],
        proj_in.at[2],
        3,
        (
            first[:, :128],
            first[:, 128:],
            scalar_row(
                image_sum,
                total(mask * image * direction),
                total(mask * direction),
                norm_own,
                total(small * small),
                image_centre,
                fit,
            ),
        ),
    )

    field_all(2).wait_recv()
    proj_all(proj_in.at[2], 3).wait_recv()
    scalars = proj_in[2, :, 2, :]
    sums = jnp.sum(scalars, axis=0, keepdims=True)
    image_mean = sums[:, 0:1] / count
    norm_old = sums[:, 3:4]
    step = norm_old / (sums[:, 1:2] - image_mean * sums[:, 2:3])
    shifts = scalars[:, 5:6] - image_mean
    small_shifts = shifts * SCALE
    spread_sum = sums[:, 4:5] + jnp.sum(
        counts * (small_shifts * small_shifts), axis=0, keepdims=True
    )
    long_step = step / SCALE
    norm_now = long_step * (long_step * spread_sum) - norm_old
    ratio = norm_now / norm_old
    pressure = pressure - step * direction
    gap = gap - step * image
    shifted = (gap - (gap_mean - step * image_mean)) * mask
    previous = direction
    direction = shifted + ratio * previous
    here = near_scalars(scalars)
    rows2 = (
        (1.0 + ratio - step * here[:, 6:7]) * rows1
        - step * gather_field(2)
        - step * (here[:, 5:6] - image_mean) * mask_rows
    )
    projs2 = (
        (1.0 + ratio - step * scalars[:, 6:7]) * projs1
        - step * proj_rows(proj_in.at[2])
        - step * shifts * mask_projs
    )
    image = operate(direction, rows2, projs2)

    send_proj(
        last_out,
        last_in,
        4,
        (
            scalar_row(
                total(mask * image),
                total(mask * image * direction),
                total(mask * direction),
                total(shifted * direction),
            ),
        ),
    )
    proj_all(last_in, 4).wait_recv()
    sums = jnp.sum(last_in[:, 0, :], axis=0, keepdims=True)
    image_mean = sums[:, 0:1] / count
    step = sums[:, 3:4] / (sums[:, 1:2] - image_mean * sums[:, 2:3])
    pressure = pressure - step * direction
    gap = gap - step * image
    for ref, value in ((pressure_out, pressure), (gap_out, gap)):
        ref[pl.ds(0, CL, stride=2), :] = value[:, :128]
        ref[pl.ds(1, CL, stride=2), :] = value[:, 128:]

    for phase in range(3):
        field_all(phase).wait_send()
    proj_all(proj0_in, 0).wait_send()
    for i in range(3):
        proj_all(proj_in.at[i], i + 1).wait_send()
    proj_all(last_in, 4).wait_send()


def shards(
    pressure_init,
    gap_height,
    active,
    self_compliance,
    near_blocks,
    near_list,
    far_list,
    source_basis,
    target_basis,
    coupling,
):
    elements = pressure_init.shape[0]
    fold_shape = (elements // 128, 128)
    vmem = pltpu.VMEM
    scratch = [
        vmem(fold_shape, F32),
        vmem(fold_shape, F32),
        vmem(fold_shape, jnp.int32),
        vmem(fold_shape, F32),
        vmem((CL, NEAR, CS, CS), BF16),
        vmem((CL, NEAR), jnp.int32),
        vmem((CL, FAR), jnp.int32),
        vmem((CL * RANK, CS), BF16),
        vmem((CL * RANK, CS), BF16),
        vmem((CL, FAR, RANK * RANK), BF16),
        vmem((CL, 128), F32),
        vmem((2 * NEAR * CL, WINDOW * 2 * CL), BF16),
        vmem((NEAR * CL, DEVICES), BF16),
        vmem((CL * RANK, DEVICES), BF16),
        vmem((CL * RANK, CS), F32),
        vmem((CS, RANK * RANK), BF16),
        vmem((RANK * RANK, CS), BF16),
        vmem((NEAR * CL, CS), F32),
        vmem((CL, RANK * RANK), F32),
        vmem((3, 2 * CL, 128), BF16),
        vmem((3, WINDOW, 2 * CL, 128), BF16),
        vmem((2, 128), F32),
        vmem((DEVICES, 2, 128), F32),
        vmem((3, 3, 128), F32),
        vmem((3, DEVICES, 3, 128), F32),
        vmem((1, 128), F32),
        vmem((DEVICES, 1, 128), F32),
        pltpu.SemaphoreType.DMA((10,)),
        pltpu.SemaphoreType.DMA((3,)),
        pltpu.SemaphoreType.DMA((3,)),
        pltpu.SemaphoreType.DMA((5,)),
        pltpu.SemaphoreType.DMA((5,)),
    ]
    pressure, gap = pl.pallas_call(
        kernel,
        out_shape=[jax.ShapeDtypeStruct(fold_shape, F32)] * 2,
        in_specs=[pl.BlockSpec(memory_space=pl.ANY)] * 10,
        out_specs=[pl.BlockSpec(memory_space=pltpu.VMEM)] * 2,
        scratch_shapes=scratch,
        compiler_params=pltpu.CompilerParams(
            collective_id=0, has_side_effects=True, vmem_limit_bytes=60 * 2**20
        ),
    )(
        pressure_init.reshape(fold_shape),
        gap_height.reshape(fold_shape),
        active.reshape(fold_shape),
        self_compliance.reshape(fold_shape),
        near_blocks,
        near_list,
        far_list,
        source_basis.reshape(CL * RANK, CS),
        target_basis.reshape(CL * RANK, CS),
        coupling,
    )
    return pressure.reshape(elements), gap.reshape(elements)


def solution(mesh):
    spec = P(("group", "member"))
    return jax.shard_map(
        shards, mesh=mesh, in_specs=(spec,) * 10, out_specs=(spec, spec), check_vma=False
    )
```

```python
import functools

import jax
import jax.numpy as jnp
from jax import lax
from jax.experimental import pallas as pl
from jax.experimental.pallas import tpu as pltpu
from jax.sharding import PartitionSpec as P

MESH = pl.DeviceIdType.MESH
F32 = jnp.float32
BF16 = jnp.bfloat16
GROUPS = 8
MEMBERS = 16
DEVICES = GROUPS * MEMBERS
CL = 8
CS = 256
RANK = 32
NEAR = 9
FAR = 27
WINDOW = 3 * MEMBERS
SCALE = 2.0**-20


def hops(slot):
    steps = (slot & 3, slot >> 2 & 3, slot >> 5)
    return sum(min(step, 4 - step) for step in steps)


FAR_FIRST = sorted(range(1, DEVICES), key=lambda slot: -hops(slot))
FIELD_FIRST = sorted(range(1, WINDOW), key=lambda slot: -hops(slot % MEMBERS))


def dot(a, b, dims=((1,), (0,))):
    return lax.dot_general(a, b, (dims, ((), ())), preferred_element_type=F32)


def split3(a):
    hi = a.astype(BF16)
    rest = a - hi.astype(F32)
    mid = rest.astype(BF16)
    low = (rest - mid.astype(F32)).astype(BF16)
    return hi, mid, low


def total(a):
    return jnp.sum(jnp.sum(a, axis=0, keepdims=True), axis=1, keepdims=True)


def kernel(
    pressure_hbm,
    height_hbm,
    active_hbm,
    self_hbm,
    near_hbm,
    near_list_hbm,
    far_list_hbm,
    source_hbm,
    target_hbm,
    coupling_hbm,
    pressure_out,
    gap_out,
    direction_out,
    image_out,
    step_out,
    pressure_v,
    height_v,
    active_v,
    self_v,
    near_v,
    near_list_v,
    far_list_v,
    source_v,
    target_v,
    coupling_v,
    near_pick,
    near_dev,
    far_pick,
    far_seg,
    spread,
    fold,
    rows_v,
    field_out,
    field_in,
    proj0_out,
    proj0_in,
    proj_out,
    proj_in,
    last_out,
    last_in,
    load_sem,
    field_send,
    field_recv,
    proj_send,
    proj_recv,
):
    g = lax.axis_index("group")
    m = lax.axis_index("member")

    def around(dy, dz):
        return lax.bitwise_and(m + 4 * dy, 12) + lax.bitwise_and(m + dz, 3)

    groups = [lax.bitwise_and(g + 2 * dx, 6) + lax.bitwise_xor(lax.bitwise_and(g, 1), dc) for dx in range(4) for dc in range(2)]
    members = [around(dy, dz) for dy in range(4) for dz in range(4)]
    sides = (g, lax.bitwise_and(g + 1, 7), lax.bitwise_and(g + 7, 7))

    def peer(slot):
        return groups[slot // MEMBERS], members[slot % MEMBERS]

    barrier = pltpu.get_barrier_semaphore()

    for slot in FAR_FIRST:
        pl.semaphore_signal(barrier, inc=1, device_id=peer(slot), device_id_type=MESH)

    pairs = (
        (pressure_hbm, pressure_v),
        (active_hbm, active_v),
        (source_hbm, source_v),
        (near_list_hbm, near_list_v),
        (far_list_hbm, far_list_v),
        (self_hbm, self_v),
        (height_hbm, height_v),
        (coupling_hbm, coupling_v),
        (target_hbm, target_v),
        (near_hbm, near_v),
    )
    loads = [pltpu.make_async_copy(a, b, load_sem.at[i]) for i, (a, b) in enumerate(pairs)]
    for load in loads:
        load.start()

    def wide(ref):
        return jnp.concatenate(
            [ref[pl.ds(0, CL, stride=2), :], ref[pl.ds(1, CL, stride=2), :]], axis=1
        )

    def tall(value):
        return jnp.concatenate([value[:, :128], value[:, 128:]], axis=0)

    row8 = lax.broadcasted_iota(jnp.int32, (CL, CS), 0)
    lane8 = lax.broadcasted_iota(jnp.int32, (CL, CS), 1)
    own = row8 == lax.shift_right_logical(lane8, 5)

    def project(value16):
        product = dot(value16, source_v[...], ((1,), (1,)))
        first = jnp.sum(jnp.where(own, product[:CL], 0.0), axis=0, keepdims=True)
        second = jnp.sum(jnp.where(own, product[CL:], 0.0), axis=0, keepdims=True)
        return first, second

    lane1 = lax.broadcasted_iota(jnp.int32, (1, 128), 1)

    def scalar_row(*values):
        row = jnp.zeros((1, 128), F32)
        for i, value in enumerate(values):
            row = jnp.where(lane1 == i, value, row)
        return row

    def field_copy(phase, slot):
        return pltpu.make_async_remote_copy(
            src_ref=field_out.at[phase],
            dst_ref=field_in.at[phase, slot],
            send_sem=field_send.at[phase],
            recv_sem=field_recv.at[phase],
            device_id=(sides[slot // MEMBERS], members[slot % MEMBERS]),
            device_id_type=MESH,
        )

    def field_all(phase):
        rest = field_in.at[phase, pl.ds(1, WINDOW - 1)]
        return pltpu.make_async_remote_copy(
            src_ref=rest,
            dst_ref=rest,
            send_sem=field_send.at[phase],
            recv_sem=field_recv.at[phase],
            device_id=peer(1),
            device_id_type=MESH,
        )

    def proj_copy(out, into, sem, slot):
        return pltpu.make_async_remote_copy(
            src_ref=out,
            dst_ref=into.at[slot],
            send_sem=proj_send.at[sem],
            recv_sem=proj_recv.at[sem],
            device_id=peer(slot),
            device_id_type=MESH,
        )

    def proj_all(into, sem):
        rest = into.at[pl.ds(1, DEVICES - 1)]
        return pltpu.make_async_remote_copy(
            src_ref=rest,
            dst_ref=rest,
            send_sem=proj_send.at[sem],
            recv_sem=proj_recv.at[sem],
            device_id=peer(1),
            device_id_type=MESH,
        )

    def send_field(phase, value):
        block = tall(value).astype(BF16)
        field_out[phase] = block
        field_in[phase, 0] = block
        for slot in FIELD_FIRST:
            field_copy(phase, slot).start()

    def send_proj(out, into, sem, rows):
        for i, row in enumerate(rows):
            out[i : i + 1, :] = row
            into[0, i : i + 1, :] = row
        for slot in FAR_FIRST:
            proj_copy(out, into, sem, slot).start()

    loads[0].wait()
    loads[1].wait()
    mask = wide(active_v).astype(F32)
    pressure = wide(pressure_v) * mask
    loads[2].wait()
    first, mask_proj = project(jnp.concatenate([pressure, mask], axis=0).astype(BF16))
    count_own = total(mask)

    loads[3].wait()
    loads[4].wait()
    near_ids = near_list_v[...]

    def member_part(ids):
        dy = lax.bitwise_and(m - lax.bitwise_and(lax.shift_right_logical(ids, 3), 12), 12)
        return dy + lax.bitwise_and(m - lax.shift_right_logical(ids, 3), 3)

    def group_part(ids):
        theirs = lax.shift_right_logical(ids, 7)
        dx = lax.bitwise_and(g - lax.bitwise_and(theirs, 6), 6)
        return (dx + lax.bitwise_and(g + theirs, 1)) * MEMBERS

    dg = lax.bitwise_and(g - lax.shift_right_logical(near_ids, 7), 7)
    near_slot = jnp.where(dg == 7, 2, dg) * MEMBERS + member_part(near_ids)
    near_row = near_slot * (2 * CL) + lax.bitwise_and(near_ids, 7)
    dev_row = group_part(near_ids) + member_part(near_ids)
    pick_iota = lax.broadcasted_iota(jnp.int32, (CL, WINDOW * 2 * CL), 1)
    dev_iota = lax.broadcasted_iota(jnp.int32, (CL, DEVICES), 1)
    low, high, dev = [], [], []
    for n in range(NEAR):
        low.append(jnp.where(pick_iota == near_row[:, n : n + 1], 1.0, 0.0))
        high.append(jnp.where(pick_iota == near_row[:, n : n + 1] + CL, 1.0, 0.0))
        dev.append(jnp.where(dev_iota == dev_row[:, n : n + 1], 1.0, 0.0))
    near_pick[...] = jnp.concatenate(low + high, axis=0).astype(BF16)
    near_dev[...] = jnp.concatenate(dev, axis=0).astype(BF16)

    far_ids = far_list_v[...]
    far_row = group_part(far_ids) + member_part(far_ids)
    far_part = lax.bitwise_and(far_ids, 7)
    part_iota = lax.shift_right_logical(lane8, 5)
    picks, parts = [], []
    for f in range(FAR):
        picks.append(jnp.where(dev_iota == far_row[:, f : f + 1], 1.0, 0.0))
        parts.append(jnp.where(part_iota == far_part[:, f : f + 1], 1.0, 0.0))
    far_pick[...] = jnp.concatenate(picks, axis=0).astype(BF16)
    far_seg[...] = jnp.concatenate(parts, axis=0)
    tall_iota = lax.bitwise_and(lax.broadcasted_iota(jnp.int32, (CS, RANK * RANK), 0), RANK - 1)
    wide_iota = lax.bitwise_and(lax.broadcasted_iota(jnp.int32, (CS, RANK * RANK), 1), RANK - 1)
    spread[...] = jnp.where(tall_iota == wide_iota, 1.0, 0.0).astype(BF16)
    tall_iota = lax.shift_right_logical(lax.broadcasted_iota(jnp.int32, (RANK * RANK, CS), 0), 5)
    wide_iota = lax.bitwise_and(lax.broadcasted_iota(jnp.int32, (RANK * RANK, CS), 1), RANK - 1)
    fold[...] = jnp.where(tall_iota == wide_iota, 1.0, 0.0).astype(BF16)
    pl.semaphore_wait(barrier, DEVICES - 1)
    send_field(0, pressure)
    send_proj(proj0_out, proj0_in, 0, (first[:, :128], first[:, 128:]))
    send_proj(
        proj_out.at[0],
        proj_in.at[0],
        1,
        (mask_proj[:, :128], mask_proj[:, 128:], scalar_row(count_own)),
    )

    for load in loads[5:]:
        load.wait()
    compliance = wide(self_v)
    height = wide(height_v)

    def turn(c, carry):
        for n in range(NEAR):
            near_v[c, n] = jnp.transpose(near_v[c, n])
        return carry

    lax.fori_loop(0, CL, turn, 0)

    row16 = lax.broadcasted_iota(jnp.int32, (2 * CL, CS), 0)

    def gather_field(phase):
        window = field_in[phase].reshape(WINDOW * 2 * CL, 128)
        picked = dot(near_pick[...], window)
        half = NEAR * CL
        return jnp.concatenate([picked[:half], picked[half:]], axis=1)

    def near_products(rows):
        rows_v[...] = rows
        products = []
        for n in range(NEAR):
            acc = jnp.zeros((2 * CL, CS), F32)
            for c in range(CL):
                row = rows_v[n * CL + c : n * CL + c + 1, :]
                left = jnp.where(row16 == c, row, 0.0).astype(BF16)
                acc = acc + dot(left, near_v[c, n])
            products.append(acc[:CL])
        return jnp.concatenate(products, axis=0)

    def slot_sum(products):
        out = products[:CL]
        for n in range(1, NEAR):
            out = out + products[n * CL : (n + 1) * CL]
        return out

    def far_sum(projected):
        picked = dot(far_pick[...], projected.astype(BF16))
        spreaded = dot((picked * far_seg[...]).astype(BF16), spread[...])
        summed = jnp.zeros((CL, RANK * RANK), F32)
        for f in range(FAR):
            summed = summed + spreaded[f * CL : (f + 1) * CL] * coupling_v[f].astype(F32)
        hi, mid, low = split3(summed)
        coupled = dot(hi, fold[...]) + (dot(mid, fold[...]) + dot(low, fold[...]))
        return dot(jnp.where(own, coupled, 0.0).astype(BF16), target_v[...])

    def operate(value, products, projected):
        narrow = value.astype(BF16).astype(F32)
        return compliance * narrow + (slot_sum(products) + far_sum(projected))

    def proj_rows(ref):
        return jnp.concatenate([ref[:, 0, :], ref[:, 1, :]], axis=1)

    def near_scalars(scalars):
        hi, mid, low = split3(scalars)
        return dot(near_dev[...], hi) + (dot(near_dev[...], mid) + dot(near_dev[...], low))

    field_all(0).wait_recv()
    rows0 = gather_field(0)
    mask_rows = jnp.where(rows0 != 0.0, 1.0, 0.0)
    near0 = near_products(rows0)
    proj_all(proj0_in, 0).wait_recv()
    gap = operate(pressure, near0, proj_rows(proj0_in)) - height

    safe_count = jnp.maximum(count_own, 1.0)
    gap_sum = total(mask * gap)
    gap_centre = gap_sum / safe_count
    local = (gap - gap_centre) * mask
    send_field(1, local)
    zeros = jnp.zeros_like(local)
    first, _ = project(jnp.concatenate([local, zeros], axis=0).astype(BF16))
    send_proj(
        proj_out.at[1],
        proj_in.at[1],
        2,
        (first[:, :128], first[:, 128:], scalar_row(gap_sum, gap_centre)),
    )

    mask_near = near_products(mask_rows)
    proj_all(proj_in.at[0], 1).wait_recv()
    mask_projs = proj_rows(proj_in.at[0])
    counts = proj_in[0, :, 2, :][:, 0:1]
    count = jnp.sum(counts, axis=0, keepdims=True)

    field_all(1).wait_recv()
    near1 = near_products(gather_field(1))
    proj_all(proj_in.at[1], 2).wait_recv()
    scalars = proj_in[1, :, 2, :]
    gap_mean = jnp.sum(scalars[:, 0:1], axis=0, keepdims=True) / count
    direction = (gap - gap_mean) * mask
    here = near_scalars(scalars)
    near1 = near1 + (here[:, 1:2] - gap_mean) * mask_near
    projs1 = proj_rows(proj_in.at[1]) + (scalars[:, 1:2] - gap_mean) * mask_projs
    image = operate(direction, near1, projs1)

    image_sum = total(mask * image)
    image_centre = image_sum / safe_count
    centred = (image - image_centre) * mask
    norm_own = total(direction * direction)
    fit = total(centred * direction) / jnp.where(norm_own > 0.0, norm_own, 1.0)
    local = centred - fit * direction
    send_field(2, local)
    first, _ = project(jnp.concatenate([local, zeros], axis=0).astype(BF16))
    small = centred * SCALE
    send_proj(
        proj_out.at[2],
        proj_in.at[2],
        3,
        (
            first[:, :128],
            first[:, 128:],
            scalar_row(
                image_sum,
                total(mask * image * direction),
                total(mask * direction),
                norm_own,
                total(small * small),
                image_centre,
                fit,
            ),
        ),
    )

    field_all(2).wait_recv()
    near2 = near_products(gather_field(2))
    proj_all(proj_in.at[2], 3).wait_recv()
    scalars = proj_in[2, :, 2, :]
    sums = jnp.sum(scalars, axis=0, keepdims=True)
    image_mean = sums[:, 0:1] / count
    norm_old = sums[:, 3:4]
    step = norm_old / (sums[:, 1:2] - image_mean * sums[:, 2:3])
    shifts = scalars[:, 5:6] - image_mean
    small_shifts = shifts * SCALE
    spread_sum = sums[:, 4:5] + jnp.sum(
        counts * (small_shifts * small_shifts), axis=0, keepdims=True
    )
    long_step = step / SCALE
    norm_now = long_step * (long_step * spread_sum) - norm_old
    ratio = norm_now / norm_old
    pressure = pressure - step * direction
    gap = gap - step * image
    shifted = (gap - (gap_mean - step * image_mean)) * mask
    previous = direction
    direction = shifted + ratio * previous
    here = near_scalars(scalars)
    near2 = (
        (1.0 + ratio - step * here[:, 6:7]) * near1
        - step * near2
        - step * (here[:, 5:6] - image_mean) * mask_near
    )
    projs2 = (
        (1.0 + ratio - step * scalars[:, 6:7]) * projs1
        - step * proj_rows(proj_in.at[2])
        - step * shifts * mask_projs
    )
    image = operate(direction, near2, projs2)

    for ref, value in (
        (pressure_out, pressure),
        (gap_out, gap),
        (direction_out, direction),
        (image_out, image),
    ):
        ref[pl.ds(0, CL, stride=2), :] = value[:, :128]
        ref[pl.ds(1, CL, stride=2), :] = value[:, 128:]

    send_proj(
        last_out,
        last_in,
        4,
        (
            scalar_row(
                total(mask * image),
                total(mask * image * direction),
                total(mask * direction),
                total(shifted * direction),
            ),
        ),
    )
    proj_all(last_in, 4).wait_recv()
    sums = jnp.sum(last_in[:, 0, :], axis=0, keepdims=True)
    image_mean = sums[:, 0:1] / count
    step = sums[:, 3:4] / (sums[:, 1:2] - image_mean * sums[:, 2:3])
    step_out[...] = jnp.broadcast_to(step, step_out.shape)

    for phase in range(3):
        field_all(phase).wait_send()
    proj_all(proj0_in, 0).wait_send()
    for i in range(3):
        proj_all(proj_in.at[i], i + 1).wait_send()
    proj_all(last_in, 4).wait_send()


def shards(
    pressure_init,
    gap_height,
    active,
    self_compliance,
    near_blocks,
    near_list,
    far_list,
    source_basis,
    target_basis,
    coupling,
):
    elements = pressure_init.shape[0]
    fold_shape = (elements // 128, 128)
    vmem = pltpu.VMEM
    scratch = [
        vmem(fold_shape, F32),
        vmem(fold_shape, F32),
        vmem(fold_shape, jnp.int32),
        vmem(fold_shape, F32),
        vmem((CL, NEAR, CS, CS), BF16),
        vmem((CL, NEAR), jnp.int32),
        vmem((CL, FAR), jnp.int32),
        vmem((CL * RANK, CS), BF16),
        vmem((CL * RANK, CS), BF16),
        vmem((FAR, CL, RANK * RANK), BF16),
        vmem((2 * NEAR * CL, WINDOW * 2 * CL), BF16),
        vmem((NEAR * CL, DEVICES), BF16),
        vmem((FAR * CL, DEVICES), BF16),
        vmem((FAR * CL, CS), F32),
        vmem((CS, RANK * RANK), BF16),
        vmem((RANK * RANK, CS), BF16),
        vmem((NEAR * CL, CS), F32),
        vmem((3, 2 * CL, 128), BF16),
        vmem((3, WINDOW, 2 * CL, 128), BF16),
        vmem((2, 128), F32),
        vmem((DEVICES, 2, 128), F32),
        vmem((3, 3, 128), F32),
        vmem((3, DEVICES, 3, 128), F32),
        vmem((1, 128), F32),
        vmem((DEVICES, 1, 128), F32),
        pltpu.SemaphoreType.DMA((10,)),
        pltpu.SemaphoreType.DMA((3,)),
        pltpu.SemaphoreType.DMA((3,)),
        pltpu.SemaphoreType.DMA((5,)),
        pltpu.SemaphoreType.DMA((5,)),
    ]
    pressure, gap, direction, image, step = pl.pallas_call(
        kernel,
        out_shape=[jax.ShapeDtypeStruct(fold_shape, F32)] * 5,
        in_specs=[pl.BlockSpec(memory_space=pl.ANY)] * 10,
        out_specs=[pl.BlockSpec(memory_space=pltpu.VMEM)] * 5,
        scratch_shapes=scratch,
        compiler_params=pltpu.CompilerParams(
            collective_id=0, has_side_effects=True, vmem_limit_bytes=60 * 2**20
        ),
    )(
        pressure_init.reshape(fold_shape),
        gap_height.reshape(fold_shape),
        active.reshape(fold_shape),
        self_compliance.reshape(fold_shape),
        near_blocks,
        near_list,
        far_list,
        source_basis.reshape(CL * RANK, CS),
        target_basis.reshape(CL * RANK, CS),
        jnp.transpose(coupling, (1, 0, 2)),
    )
    pressure = pressure - step * direction
    gap = gap - step * image
    return pressure.reshape(elements), gap.reshape(elements)


def solution(mesh):
    spec = P(("group", "member"))
    return jax.shard_map(
        shards, mesh=mesh, in_specs=(spec,) * 10, out_specs=(spec, spec), check_vma=False
    )
```

```python
import functools

import jax
import jax.numpy as jnp
from jax import lax
from jax.experimental import pallas as pl
from jax.experimental.pallas import tpu as pltpu
from jax.sharding import PartitionSpec as P

MESH = pl.DeviceIdType.MESH
F32 = jnp.float32
BF16 = jnp.bfloat16
GROUPS = 8
MEMBERS = 16
DEVICES = GROUPS * MEMBERS
CL = 8
CS = 256
RANK = 32
NEAR = 9
FAR = 27
WINDOW = 3 * MEMBERS
SCALE = 2.0**-20


def hops(slot):
    steps = (slot & 3, slot >> 2 & 3, slot >> 5)
    return sum(min(step, 4 - step) for step in steps)


FAR_FIRST = sorted(range(1, DEVICES), key=lambda slot: -hops(slot))
FIELD_FIRST = sorted(range(MEMBERS), key=lambda slot: -hops(slot))


def dot(a, b, dims=((1,), (0,))):
    return lax.dot_general(a, b, (dims, ((), ())), preferred_element_type=F32)


def split3(a):
    hi = a.astype(BF16)
    rest = a - hi.astype(F32)
    mid = rest.astype(BF16)
    low = (rest - mid.astype(F32)).astype(BF16)
    return hi, mid, low


def total(a):
    return jnp.sum(jnp.sum(a, axis=0, keepdims=True), axis=1, keepdims=True)


def kernel(
    pressure_hbm,
    height_hbm,
    active_hbm,
    self_hbm,
    near_hbm,
    near_list_hbm,
    far_list_hbm,
    source_hbm,
    target_hbm,
    coupling_hbm,
    pressure_out,
    gap_out,
    direction_out,
    image_out,
    step_out,
    pressure_v,
    height_v,
    active_v,
    self_v,
    near_v,
    near_list_v,
    far_list_v,
    source_v,
    target_v,
    coupling_v,
    near_pick,
    near_dev,
    far_pick,
    far_seg,
    spread,
    fold,
    rows_v,
    field_out,
    field_in,
    proj0_out,
    proj0_in,
    proj_out,
    proj_in,
    last_out,
    last_in,
    load_sem,
    field_send,
    field_recv,
    proj_send,
    proj_recv,
):
    g = lax.axis_index("group")
    m = lax.axis_index("member")

    def around(dy, dz):
        return lax.bitwise_and(m + 4 * dy, 12) + lax.bitwise_and(m + dz, 3)

    groups = [lax.bitwise_and(g + 2 * dx, 6) + lax.bitwise_xor(lax.bitwise_and(g, 1), dc) for dx in range(4) for dc in range(2)]
    members = [around(dy, dz) for dy in range(4) for dz in range(4)]

    def peer(slot):
        return groups[slot // MEMBERS], members[slot % MEMBERS]

    barrier = pltpu.get_barrier_semaphore()

    for slot in FAR_FIRST:
        pl.semaphore_signal(barrier, inc=1, device_id=peer(slot), device_id_type=MESH)

    pairs = (
        (pressure_hbm, pressure_v),
        (active_hbm, active_v),
        (source_hbm, source_v),
        (near_list_hbm, near_list_v),
        (far_list_hbm, far_list_v),
        (self_hbm, self_v),
        (height_hbm, height_v),
        (coupling_hbm, coupling_v),
        (target_hbm, target_v),
        (near_hbm, near_v),
    )
    loads = [pltpu.make_async_copy(a, b, load_sem.at[i]) for i, (a, b) in enumerate(pairs)]
    for load in loads:
        load.start()

    def wide(ref):
        return jnp.concatenate(
            [ref[pl.ds(0, CL, stride=2), :], ref[pl.ds(1, CL, stride=2), :]], axis=1
        )

    def tall(value):
        return jnp.concatenate([value[:, :128], value[:, 128:]], axis=0)

    row8 = lax.broadcasted_iota(jnp.int32, (CL, CS), 0)
    lane8 = lax.broadcasted_iota(jnp.int32, (CL, CS), 1)
    own = row8 == lax.shift_right_logical(lane8, 5)

    def project(value16):
        product = dot(value16, source_v[...], ((1,), (1,)))
        first = jnp.sum(jnp.where(own, product[:CL], 0.0), axis=0, keepdims=True)
        second = jnp.sum(jnp.where(own, product[CL:], 0.0), axis=0, keepdims=True)
        return first, second

    def project_fine(value):
        high = value.astype(BF16).astype(F32)
        first, second = project(jnp.concatenate([high, value - high], axis=0).astype(BF16))
        return first + second

    lane1 = lax.broadcasted_iota(jnp.int32, (1, 128), 1)

    def scalar_row(*values):
        row = jnp.zeros((1, 128), F32)
        for i, value in enumerate(values):
            row = jnp.where(lane1 == i, value, row)
        return row

    odd = lax.bitwise_and(g, 1)
    partner = lax.bitwise_xor(g, 1)
    across = lax.bitwise_and(g - 1 + 2 * odd, 7)

    def field_copy(phase, kind, src, start, to, count=1):
        return pltpu.make_async_remote_copy(
            src_ref=src,
            dst_ref=field_in.at[phase, pl.ds(start, count)],
            send_sem=field_send.at[phase, kind],
            recv_sem=field_recv.at[phase, kind],
            device_id=to,
            device_id_type=MESH,
        )

    def field_all(phase, kind):
        start, count = ((1, MEMBERS - 1), (MEMBERS, MEMBERS), (2 * MEMBERS, MEMBERS))[kind]
        rest = field_in.at[phase, pl.ds(start, count)]
        return field_copy(phase, kind, rest, start, peer(1), count)

    def forward(phase):
        field_all(phase, 0).wait_recv()
        whole = field_in.at[phase, pl.ds(0, MEMBERS)]
        field_copy(phase, 2, whole, (1 + odd) * MEMBERS, (partner, m), MEMBERS).start()

    def field_here(phase):
        forward(phase)
        field_all(phase, 1).wait_recv()
        field_all(phase, 2).wait_recv()

    def proj_copy(out, into, sem, slot):
        return pltpu.make_async_remote_copy(
            src_ref=out,
            dst_ref=into.at[pl.ds(slot * out.shape[0], out.shape[0])],
            send_sem=proj_send.at[sem],
            recv_sem=proj_recv.at[sem],
            device_id=peer(slot),
            device_id_type=MESH,
        )

    def proj_all(into, sem):
        each = into.shape[0] // DEVICES
        rest = into.at[pl.ds(each, (DEVICES - 1) * each)]
        return pltpu.make_async_remote_copy(
            src_ref=rest,
            dst_ref=rest,
            send_sem=proj_send.at[sem],
            recv_sem=proj_recv.at[sem],
            device_id=peer(1),
            device_id_type=MESH,
        )

    def send_field(phase, value):
        block = tall(value).astype(BF16)
        field_out[phase, 0] = block
        field_in[phase, 0] = block
        src = field_out.at[phase]
        for slot in FIELD_FIRST:
            if slot:
                field_copy(phase, 0, src, slot, (g, members[slot])).start()
        for slot in FIELD_FIRST:
            field_copy(phase, 1, src, (2 - odd) * MEMBERS + slot, (across, members[slot])).start()

    def send_proj(out, into, sem, rows):
        for i, row in enumerate(rows):
            out[i : i + 1, :] = row
            into[i : i + 1, :] = row
        for slot in FAR_FIRST:
            proj_copy(out, into, sem, slot).start()

    loads[0].wait()
    loads[1].wait()
    mask = wide(active_v).astype(F32)
    pressure = wide(pressure_v) * mask
    loads[2].wait()
    first, mask_proj = project(jnp.concatenate([pressure, mask], axis=0).astype(BF16))
    count_own = total(mask)

    loads[3].wait()
    loads[4].wait()
    near_ids = near_list_v[...]

    def member_part(ids):
        dy = lax.bitwise_and(m - lax.bitwise_and(lax.shift_right_logical(ids, 3), 12), 12)
        return dy + lax.bitwise_and(m - lax.shift_right_logical(ids, 3), 3)

    def group_part(ids):
        theirs = lax.shift_right_logical(ids, 7)
        dx = lax.bitwise_and(g - lax.bitwise_and(theirs, 6), 6)
        return (dx + lax.bitwise_and(g + theirs, 1)) * MEMBERS

    dg = lax.bitwise_and(g - lax.shift_right_logical(near_ids, 7), 7)
    near_slot = jnp.where(dg == 7, 2, dg) * MEMBERS + member_part(near_ids)
    near_row = near_slot * (2 * CL) + lax.bitwise_and(near_ids, 7)
    dev_row = group_part(near_ids) + member_part(near_ids)
    pick_iota = lax.broadcasted_iota(jnp.int32, (CL, WINDOW * 2 * CL), 1)
    dev_iota = lax.broadcasted_iota(jnp.int32, (CL, DEVICES), 1)
    low, high, dev = [], [], []
    for n in range(NEAR):
        low.append(jnp.where(pick_iota == near_row[:, n : n + 1], 1.0, 0.0))
        high.append(jnp.where(pick_iota == near_row[:, n : n + 1] + CL, 1.0, 0.0))
        dev.append(jnp.where(dev_iota == dev_row[:, n : n + 1], 1.0, 0.0))
    near_pick[...] = jnp.concatenate(low + high, axis=0).astype(BF16)
    near_dev[...] = jnp.concatenate(dev, axis=0).astype(BF16)

    far_ids = far_list_v[...]
    far_row = group_part(far_ids) + member_part(far_ids)
    far_part = lax.bitwise_and(far_ids, 7)
    part_iota = lax.shift_right_logical(lane8, 5)
    picks, parts = [], []
    for f in range(FAR):
        picks.append(jnp.where(dev_iota == far_row[:, f : f + 1], 1.0, 0.0))
        parts.append(jnp.where(part_iota == far_part[:, f : f + 1], 1.0, 0.0))
    far_pick[...] = jnp.concatenate(picks, axis=0).astype(BF16)
    far_seg[...] = jnp.concatenate(parts, axis=0)
    tall_iota = lax.bitwise_and(lax.broadcasted_iota(jnp.int32, (CS, RANK * RANK), 0), RANK - 1)
    wide_iota = lax.bitwise_and(lax.broadcasted_iota(jnp.int32, (CS, RANK * RANK), 1), RANK - 1)
    spread[...] = jnp.where(tall_iota == wide_iota, 1.0, 0.0).astype(BF16)
    tall_iota = lax.shift_right_logical(lax.broadcasted_iota(jnp.int32, (RANK * RANK, CS), 0), 5)
    wide_iota = lax.bitwise_and(lax.broadcasted_iota(jnp.int32, (RANK * RANK, CS), 1), RANK - 1)
    fold[...] = jnp.where(tall_iota == wide_iota, 1.0, 0.0).astype(BF16)
    pl.semaphore_wait(barrier, DEVICES - 1)
    send_field(0, pressure)
    send_proj(proj0_out, proj0_in, 0, (first[:, :128], first[:, 128:]))
    send_proj(
        proj_out.at[0],
        proj_in.at[0],
        1,
        (mask_proj[:, :128], mask_proj[:, 128:], scalar_row(count_own)),
    )

    for load in loads[5:]:
        load.wait()
    compliance = wide(self_v)
    height = wide(height_v)

    def turn(c, carry):
        for n in range(NEAR):
            near_v[c, n] = jnp.transpose(near_v[c, n])
        return carry

    lax.fori_loop(0, CL, turn, 0)

    row16 = lax.broadcasted_iota(jnp.int32, (2 * CL, CS), 0)

    def gather_field(phase):
        window = field_in[phase].reshape(WINDOW * 2 * CL, 128)
        picked = dot(near_pick[...], window)
        half = NEAR * CL
        return jnp.concatenate([picked[:half], picked[half:]], axis=1)

    def near_products(rows):
        rows_v[...] = rows
        products = []
        for n in range(NEAR):
            acc = jnp.zeros((2 * CL, CS), F32)
            for c in range(CL):
                row = rows_v[n * CL + c : n * CL + c + 1, :]
                left = jnp.where(row16 == c, row, 0.0).astype(BF16)
                acc = acc + dot(left, near_v[c, n])
            products.append(acc[:CL])
        return jnp.concatenate(products, axis=0)

    def slot_sum(products):
        out = products[:CL]
        for n in range(1, NEAR):
            out = out + products[n * CL : (n + 1) * CL]
        return out

    def far_sum(projected):
        picked = dot(far_pick[...], projected.astype(BF16))
        spreaded = dot((picked * far_seg[...]).astype(BF16), spread[...])
        summed = jnp.zeros((CL, RANK * RANK), F32)
        for f in range(FAR):
            summed = summed + spreaded[f * CL : (f + 1) * CL] * coupling_v[f].astype(F32)
        high = summed.astype(BF16).astype(F32)
        both = dot(jnp.concatenate([high, summed - high], axis=0).astype(BF16), fold[...])
        coupled = both[:CL] + both[CL:]
        return dot(jnp.where(own, coupled, 0.0).astype(BF16), target_v[...])

    def operate(value, products, projected):
        narrow = value.astype(BF16).astype(F32)
        return compliance * narrow + (slot_sum(products) + far_sum(projected))

    def rows_of(ref, i):
        return ref[pl.ds(i, DEVICES, stride=ref.shape[0] // DEVICES), :]

    def proj_rows(ref):
        return jnp.concatenate([rows_of(ref, 0), rows_of(ref, 1)], axis=1)

    def near_scalars(scalars):
        picked = dot(near_dev[...], jnp.concatenate(split3(scalars), axis=1))
        return picked[:, :128] + (picked[:, 128:256] + picked[:, 256:])

    field_here(0)
    rows0 = gather_field(0)
    mask_rows = jnp.where(rows0 != 0.0, 1.0, 0.0)
    near0 = near_products(rows0)
    proj_all(proj0_in, 0).wait_recv()
    gap = operate(pressure, near0, proj_rows(proj0_in)) - height

    safe_count = jnp.maximum(count_own, 1.0)
    gap_sum = total(mask * gap)
    gap_centre = gap_sum / safe_count
    local = (gap - gap_centre) * mask
    send_field(1, local)
    first = project_fine(local)
    send_proj(
        proj_out.at[1],
        proj_in.at[1],
        2,
        (first[:, :128], first[:, 128:], scalar_row(gap_sum, gap_centre)),
    )

    mask_near = near_products(mask_rows)
    proj_all(proj_in.at[0], 1).wait_recv()
    mask_projs = proj_rows(proj_in.at[0])
    counts = rows_of(proj_in.at[0], 2)[:, 0:1]
    count = jnp.sum(counts, axis=0, keepdims=True)

    field_here(1)
    near1 = near_products(gather_field(1))
    proj_all(proj_in.at[1], 2).wait_recv()
    scalars = rows_of(proj_in.at[1], 2)
    gap_mean = jnp.sum(scalars[:, 0:1], axis=0, keepdims=True) / count
    direction = (gap - gap_mean) * mask
    here = near_scalars(scalars)
    near1 = near1 + (here[:, 1:2] - gap_mean) * mask_near
    projs1 = proj_rows(proj_in.at[1]) + (scalars[:, 1:2] - gap_mean) * mask_projs
    image = operate(direction, near1, projs1)

    image_sum = total(mask * image)
    image_centre = image_sum / safe_count
    centred = (image - image_centre) * mask
    norm_own = total(direction * direction)
    direction_sum = total(mask * direction)
    cross = total(mask * image * direction)
    fit = (cross - image_centre * direction_sum) / jnp.where(norm_own > 0.0, norm_own, 1.0)
    local = centred - fit * direction
    send_field(2, local)
    first = project_fine(local)
    small = centred * SCALE
    send_proj(
        proj_out.at[2],
        proj_in.at[2],
        3,
        (
            first[:, :128],
            first[:, 128:],
            scalar_row(
                image_sum,
                cross,
                direction_sum,
                norm_own,
                total(small * small),
                image_centre,
                fit,
            ),
        ),
    )

    field_here(2)
    near2 = near_products(gather_field(2))
    proj_all(proj_in.at[2], 3).wait_recv()
    scalars = rows_of(proj_in.at[2], 2)
    sums = jnp.sum(scalars, axis=0, keepdims=True)
    image_mean = sums[:, 0:1] / count
    norm_old = sums[:, 3:4]
    step = norm_old / (sums[:, 1:2] - image_mean * sums[:, 2:3])
    shifts = scalars[:, 5:6] - image_mean
    small_shifts = shifts * SCALE
    spread_sum = sums[:, 4:5] + jnp.sum(
        counts * (small_shifts * small_shifts), axis=0, keepdims=True
    )
    long_step = step / SCALE
    norm_now = long_step * (long_step * spread_sum) - norm_old
    ratio = norm_now / norm_old
    pressure = pressure - step * direction
    gap = gap - step * image
    shifted = (gap - (gap_mean - step * image_mean)) * mask
    previous = direction
    direction = shifted + ratio * previous
    here = near_scalars(scalars)
    near2 = (
        (1.0 + ratio - step * here[:, 6:7]) * near1
        - step * near2
        - step * (here[:, 5:6] - image_mean) * mask_near
    )
    projs2 = (
        (1.0 + ratio - step * scalars[:, 6:7]) * projs1
        - step * proj_rows(proj_in.at[2])
        - step * shifts * mask_projs
    )
    image = operate(direction, near2, projs2)

    for ref, value in (
        (pressure_out, pressure),
        (gap_out, gap),
        (direction_out, direction),
        (image_out, image),
    ):
        ref[pl.ds(0, CL, stride=2), :] = value[:, :128]
        ref[pl.ds(1, CL, stride=2), :] = value[:, 128:]

    send_proj(
        last_out,
        last_in,
        4,
        (
            scalar_row(
                total(mask * image),
                total(mask * image * direction),
                total(mask * direction),
                total(shifted * direction),
            ),
        ),
    )
    proj_all(last_in, 4).wait_recv()
    sums = jnp.sum(last_in[...], axis=0, keepdims=True)
    image_mean = sums[:, 0:1] / count
    step = sums[:, 3:4] / (sums[:, 1:2] - image_mean * sums[:, 2:3])
    step_out[...] = jnp.broadcast_to(step, step_out.shape)

    for phase in range(3):
        for kind in range(3):
            field_all(phase, kind).wait_send()
    proj_all(proj0_in, 0).wait_send()
    for i in range(3):
        proj_all(proj_in.at[i], i + 1).wait_send()
    proj_all(last_in, 4).wait_send()


def shards(
    pressure_init,
    gap_height,
    active,
    self_compliance,
    near_blocks,
    near_list,
    far_list,
    source_basis,
    target_basis,
    coupling,
):
    elements = pressure_init.shape[0]
    fold_shape = (elements // 128, 128)
    vmem = pltpu.VMEM
    scratch = [
        vmem(fold_shape, F32),
        vmem(fold_shape, F32),
        vmem(fold_shape, jnp.int32),
        vmem(fold_shape, F32),
        vmem((CL, NEAR, CS, CS), BF16),
        vmem((CL, NEAR), jnp.int32),
        vmem((CL, FAR), jnp.int32),
        vmem((CL * RANK, CS), BF16),
        vmem((CL * RANK, CS), BF16),
        vmem((FAR, CL, RANK * RANK), BF16),
        vmem((2 * NEAR * CL, WINDOW * 2 * CL), BF16),
        vmem((NEAR * CL, DEVICES), BF16),
        vmem((FAR * CL, DEVICES), BF16),
        vmem((FAR * CL, CS), F32),
        vmem((CS, RANK * RANK), BF16),
        vmem((RANK * RANK, CS), BF16),
        vmem((NEAR * CL, CS), F32),
        vmem((3, 1, 2 * CL, 128), BF16),
        vmem((3, WINDOW, 2 * CL, 128), BF16),
        vmem((2, 128), F32),
        vmem((DEVICES * 2, 128), F32),
        vmem((3, 3, 128), F32),
        vmem((3, DEVICES * 3, 128), F32),
        vmem((1, 128), F32),
        vmem((DEVICES, 128), F32),
        pltpu.SemaphoreType.DMA((10,)),
        pltpu.SemaphoreType.DMA((3, 3)),
        pltpu.SemaphoreType.DMA((3, 3)),
        pltpu.SemaphoreType.DMA((5,)),
        pltpu.SemaphoreType.DMA((5,)),
    ]
    pressure, gap, direction, image, step = pl.pallas_call(
        kernel,
        out_shape=[jax.ShapeDtypeStruct(fold_shape, F32)] * 5,
        in_specs=[pl.BlockSpec(memory_space=pl.ANY)] * 10,
        out_specs=[pl.BlockSpec(memory_space=pltpu.VMEM)] * 5,
        scratch_shapes=scratch,
        compiler_params=pltpu.CompilerParams(
            collective_id=0, has_side_effects=True, vmem_limit_bytes=60 * 2**20
        ),
    )(
        pressure_init.reshape(fold_shape),
        gap_height.reshape(fold_shape),
        active.reshape(fold_shape),
        self_compliance.reshape(fold_shape),
        near_blocks,
        near_list,
        far_list,
        source_basis.reshape(CL * RANK, CS),
        target_basis.reshape(CL * RANK, CS),
        jnp.transpose(coupling, (1, 0, 2)),
    )
    pressure = pressure - step * direction
    gap = gap - step * image
    return pressure.reshape(elements), gap.reshape(elements)


def solution(mesh):
    spec = P(("group", "member"))
    return jax.shard_map(
        shards, mesh=mesh, in_specs=(spec,) * 10, out_specs=(spec, spec), check_vma=False
    )
```

```python
import functools

import jax
import jax.numpy as jnp
from jax import lax
from jax.experimental import pallas as pl
from jax.experimental.pallas import tpu as pltpu
from jax.sharding import PartitionSpec as P

MESH = pl.DeviceIdType.MESH
F32 = jnp.float32
BF16 = jnp.bfloat16
GROUPS = 8
MEMBERS = 16
DEVICES = GROUPS * MEMBERS
CL = 8
CS = 256
RANK = 32
NEAR = 9
FAR = 27
WINDOW = 3 * MEMBERS
SCALE = 2.0**-20


def hops(slot):
    steps = (slot & 3, slot >> 2 & 3, slot >> 5)
    return sum(min(step, 4 - step) for step in steps)


FAR_FIRST = sorted(range(1, DEVICES), key=lambda slot: -hops(slot))
FIELD_FIRST = sorted(range(MEMBERS), key=lambda slot: -hops(slot))


def dot(a, b, dims=((1,), (0,))):
    return lax.dot_general(a, b, (dims, ((), ())), preferred_element_type=F32)


def split3(a):
    hi = a.astype(BF16)
    rest = a - hi.astype(F32)
    mid = rest.astype(BF16)
    low = (rest - mid.astype(F32)).astype(BF16)
    return hi, mid, low


def total(a):
    return jnp.sum(jnp.sum(a, axis=0, keepdims=True), axis=1, keepdims=True)


def kernel(
    pressure_hbm,
    height_hbm,
    active_hbm,
    self_hbm,
    near_hbm,
    near_list_hbm,
    far_list_hbm,
    source_hbm,
    target_hbm,
    coupling_hbm,
    pressure_out,
    gap_out,
    direction_out,
    image_out,
    step_out,
    pressure_v,
    height_v,
    active_v,
    self_v,
    near_v,
    near_list_v,
    far_list_v,
    source_v,
    target_v,
    coupling_v,
    near_pick,
    near_dev,
    far_pick,
    far_seg,
    spread,
    fold,
    rows_v,
    field_out,
    field_in,
    proj0_out,
    proj0_in,
    proj_out,
    proj_in,
    last_out,
    last_in,
    load_sem,
    field_send,
    field_recv,
    proj_send,
    proj_recv,
):
    g = lax.axis_index("group")
    m = lax.axis_index("member")

    def around(dy, dz):
        return lax.bitwise_and(m + 4 * dy, 12) + lax.bitwise_and(m + dz, 3)

    groups = [lax.bitwise_and(g + 2 * dx, 6) + lax.bitwise_xor(lax.bitwise_and(g, 1), dc) for dx in range(4) for dc in range(2)]
    members = [around(dy, dz) for dy in range(4) for dz in range(4)]

    def peer(slot):
        return groups[slot // MEMBERS], members[slot % MEMBERS]

    barrier = pltpu.get_barrier_semaphore()

    for slot in FAR_FIRST:
        pl.semaphore_signal(barrier, inc=1, device_id=peer(slot), device_id_type=MESH)

    pairs = (
        (pressure_hbm, pressure_v),
        (active_hbm, active_v),
        (source_hbm, source_v),
        (near_list_hbm, near_list_v),
        (far_list_hbm, far_list_v),
        (self_hbm, self_v),
        (height_hbm, height_v),
        (coupling_hbm, coupling_v),
        (target_hbm, target_v),
        (near_hbm, near_v),
    )
    loads = [pltpu.make_async_copy(a, b, load_sem.at[i]) for i, (a, b) in enumerate(pairs)]
    for load in loads:
        load.start()

    def wide(ref):
        return jnp.concatenate(
            [ref[pl.ds(0, CL, stride=2), :], ref[pl.ds(1, CL, stride=2), :]], axis=1
        )

    def tall(value):
        return jnp.concatenate([value[:, :128], value[:, 128:]], axis=0)

    row8 = lax.broadcasted_iota(jnp.int32, (CL, CS), 0)
    lane8 = lax.broadcasted_iota(jnp.int32, (CL, CS), 1)
    own = row8 == lax.shift_right_logical(lane8, 5)

    def project(value16):
        product = dot(value16, source_v[...], ((1,), (1,)))
        first = jnp.sum(jnp.where(own, product[:CL], 0.0), axis=0, keepdims=True)
        second = jnp.sum(jnp.where(own, product[CL:], 0.0), axis=0, keepdims=True)
        return first, second

    def project_fine(value):
        high = value.astype(BF16).astype(F32)
        first, second = project(jnp.concatenate([high, value - high], axis=0).astype(BF16))
        return first + second

    lane1 = lax.broadcasted_iota(jnp.int32, (1, 128), 1)

    def scalar_row(*values):
        row = jnp.zeros((1, 128), F32)
        for i, value in enumerate(values):
            row = jnp.where(lane1 == i, value, row)
        return row

    odd = lax.bitwise_and(g, 1)
    partner = lax.bitwise_xor(g, 1)
    across = lax.bitwise_and(g - 1 + 2 * odd, 7)

    def field_copy(phase, kind, src, start, to, count=1):
        return pltpu.make_async_remote_copy(
            src_ref=src,
            dst_ref=field_in.at[phase, pl.ds(start, count)],
            send_sem=field_send.at[phase, kind],
            recv_sem=field_recv.at[phase, kind],
            device_id=to,
            device_id_type=MESH,
        )

    def field_all(phase, kind):
        start, count = ((1, MEMBERS - 1), (MEMBERS, MEMBERS), (2 * MEMBERS, MEMBERS))[kind]
        rest = field_in.at[phase, pl.ds(start, count)]
        return field_copy(phase, kind, rest, start, peer(1), count)

    def forward(phase):
        field_all(phase, 0).wait_recv()
        whole = field_in.at[phase, pl.ds(0, MEMBERS)]
        field_copy(phase, 2, whole, (1 + odd) * MEMBERS, (partner, m), MEMBERS).start()

    def field_here(phase):
        forward(phase)
        field_all(phase, 1).wait_recv()
        field_all(phase, 2).wait_recv()

    def proj_copy(out, into, sem, slot):
        return pltpu.make_async_remote_copy(
            src_ref=out,
            dst_ref=into.at[pl.ds(slot * out.shape[0], out.shape[0])],
            send_sem=proj_send.at[sem],
            recv_sem=proj_recv.at[sem],
            device_id=peer(slot),
            device_id_type=MESH,
        )

    def proj_all(into, sem):
        each = into.shape[0] // DEVICES
        rest = into.at[pl.ds(each, (DEVICES - 1) * each)]
        return pltpu.make_async_remote_copy(
            src_ref=rest,
            dst_ref=rest,
            send_sem=proj_send.at[sem],
            recv_sem=proj_recv.at[sem],
            device_id=peer(1),
            device_id_type=MESH,
        )

    def send_field(phase, value):
        block = tall(value).astype(BF16)
        field_out[phase, 0] = block
        field_in[phase, 0] = block
        src = field_out.at[phase]
        for slot in FIELD_FIRST:
            if slot:
                field_copy(phase, 0, src, slot, (g, members[slot])).start()
        for slot in FIELD_FIRST:
            field_copy(phase, 1, src, (2 - odd) * MEMBERS + slot, (across, members[slot])).start()

    def send_proj(out, into, sem, rows):
        for i, row in enumerate(rows):
            out[i : i + 1, :] = row
            into[i : i + 1, :] = row
        for slot in FAR_FIRST:
            proj_copy(out, into, sem, slot).start()

    loads[0].wait()
    loads[1].wait()
    mask = wide(active_v).astype(F32)
    pressure = wide(pressure_v) * mask
    loads[2].wait()
    first, mask_proj = project(jnp.concatenate([pressure, mask], axis=0).astype(BF16))
    count_own = total(mask)

    loads[3].wait()
    loads[4].wait()
    near_ids = near_list_v[...]

    def member_part(ids):
        dy = lax.bitwise_and(m - lax.bitwise_and(lax.shift_right_logical(ids, 3), 12), 12)
        return dy + lax.bitwise_and(m - lax.shift_right_logical(ids, 3), 3)

    def group_part(ids):
        theirs = lax.shift_right_logical(ids, 7)
        dx = lax.bitwise_and(g - lax.bitwise_and(theirs, 6), 6)
        return (dx + lax.bitwise_and(g + theirs, 1)) * MEMBERS

    dg = lax.bitwise_and(g - lax.shift_right_logical(near_ids, 7), 7)
    near_slot = jnp.where(dg == 7, 2, dg) * MEMBERS + member_part(near_ids)
    near_row = near_slot * (2 * CL) + lax.bitwise_and(near_ids, 7)
    dev_row = group_part(near_ids) + member_part(near_ids)
    pick_iota = lax.broadcasted_iota(jnp.int32, (CL, WINDOW * 2 * CL), 1)
    dev_iota = lax.broadcasted_iota(jnp.int32, (CL, DEVICES), 1)
    low, high, dev = [], [], []
    for n in range(NEAR):
        low.append(jnp.where(pick_iota == near_row[:, n : n + 1], 1.0, 0.0))
        high.append(jnp.where(pick_iota == near_row[:, n : n + 1] + CL, 1.0, 0.0))
        dev.append(jnp.where(dev_iota == dev_row[:, n : n + 1], 1.0, 0.0))
    near_pick[...] = jnp.concatenate(low + high, axis=0).astype(BF16)
    near_dev[...] = jnp.concatenate(dev, axis=0).astype(BF16)

    far_ids = far_list_v[...]
    far_row = group_part(far_ids) + member_part(far_ids)
    far_part = lax.bitwise_and(far_ids, 7)
    part_iota = lax.shift_right_logical(lane8, 5)
    picks, parts = [], []
    for f in range(FAR):
        picks.append(jnp.where(dev_iota == far_row[:, f : f + 1], 1.0, 0.0))
        parts.append(jnp.where(part_iota == far_part[:, f : f + 1], 1.0, 0.0))
    far_pick[...] = jnp.concatenate(picks, axis=0).astype(BF16)
    far_seg[...] = jnp.concatenate(parts, axis=0)
    tall_iota = lax.bitwise_and(lax.broadcasted_iota(jnp.int32, (CS, RANK * RANK), 0), RANK - 1)
    wide_iota = lax.bitwise_and(lax.broadcasted_iota(jnp.int32, (CS, RANK * RANK), 1), RANK - 1)
    spread[...] = jnp.where(tall_iota == wide_iota, 1.0, 0.0).astype(BF16)
    tall_iota = lax.shift_right_logical(lax.broadcasted_iota(jnp.int32, (RANK * RANK, CS), 0), 5)
    wide_iota = lax.bitwise_and(lax.broadcasted_iota(jnp.int32, (RANK * RANK, CS), 1), RANK - 1)
    fold[...] = jnp.where(tall_iota == wide_iota, 1.0, 0.0).astype(BF16)
    pl.semaphore_wait(barrier, DEVICES - 1)
    send_field(0, pressure)
    send_proj(proj0_out, proj0_in, 0, (first[:, :128], first[:, 128:]))

    for load in loads[5:]:
        load.wait()
    compliance = wide(self_v)
    height = wide(height_v)

    def turn(c, carry):
        for n in range(NEAR):
            near_v[c, n] = jnp.transpose(near_v[c, n])
        return carry

    lax.fori_loop(0, CL, turn, 0)

    row16 = lax.broadcasted_iota(jnp.int32, (2 * CL, CS), 0)

    def gather_field(phase):
        window = field_in[phase].reshape(WINDOW * 2 * CL, 128)
        picked = dot(near_pick[...], window)
        half = NEAR * CL
        return jnp.concatenate([picked[:half], picked[half:]], axis=1)

    def near_products(rows):
        rows_v[...] = rows
        products = []
        for n in range(NEAR):
            acc = jnp.zeros((2 * CL, CS), F32)
            for c in range(CL):
                row = rows_v[n * CL + c : n * CL + c + 1, :]
                left = jnp.where(row16 == c, row, 0.0).astype(BF16)
                acc = acc + dot(left, near_v[c, n])
            products.append(acc[:CL])
        return jnp.concatenate(products, axis=0)

    def slot_sum(products):
        out = products[:CL]
        for n in range(1, NEAR):
            out = out + products[n * CL : (n + 1) * CL]
        return out

    def far_sum(projected):
        picked = dot(far_pick[...], projected.astype(BF16))
        spreaded = dot((picked * far_seg[...]).astype(BF16), spread[...])
        summed = jnp.zeros((CL, RANK * RANK), F32)
        for f in range(FAR):
            summed = summed + spreaded[f * CL : (f + 1) * CL] * coupling_v[f].astype(F32)
        high = summed.astype(BF16).astype(F32)
        both = dot(jnp.concatenate([high, summed - high], axis=0).astype(BF16), fold[...])
        coupled = both[:CL] + both[CL:]
        return dot(jnp.where(own, coupled, 0.0).astype(BF16), target_v[...])

    def operate(value, products, projected):
        narrow = value.astype(BF16).astype(F32)
        return compliance * narrow + (slot_sum(products) + far_sum(projected))

    def rows_of(ref, i):
        return ref[pl.ds(i, DEVICES, stride=ref.shape[0] // DEVICES), :]

    def proj_rows(ref):
        return jnp.concatenate([rows_of(ref, 0), rows_of(ref, 1)], axis=1)

    def near_scalars(scalars):
        picked = dot(near_dev[...], jnp.concatenate(split3(scalars), axis=1))
        return picked[:, :128] + (picked[:, 128:256] + picked[:, 256:])

    field_here(0)
    rows0 = gather_field(0)
    mask_rows = jnp.where(rows0 != 0.0, 1.0, 0.0)
    send_proj(
        proj_out.at[0],
        proj_in.at[0],
        1,
        (mask_proj[:, :128], mask_proj[:, 128:], scalar_row(count_own)),
    )
    near0 = near_products(rows0)
    proj_all(proj0_in, 0).wait_recv()
    gap = operate(pressure, near0, proj_rows(proj0_in)) - height

    safe_count = jnp.maximum(count_own, 1.0)
    gap_sum = total(mask * gap)
    gap_centre = gap_sum / safe_count
    local = (gap - gap_centre) * mask
    send_field(1, local)
    first = project_fine(local)
    send_proj(
        proj_out.at[1],
        proj_in.at[1],
        2,
        (first[:, :128], first[:, 128:], scalar_row(gap_sum, gap_centre)),
    )

    mask_near = near_products(mask_rows)
    proj_all(proj_in.at[0], 1).wait_recv()
    mask_projs = proj_rows(proj_in.at[0])
    counts = rows_of(proj_in.at[0], 2)[:, 0:1]
    count = jnp.sum(counts, axis=0, keepdims=True)

    field_here(1)
    near1 = near_products(gather_field(1))
    proj_all(proj_in.at[1], 2).wait_recv()
    scalars = rows_of(proj_in.at[1], 2)
    gap_mean = jnp.sum(scalars[:, 0:1], axis=0, keepdims=True) / count
    direction = (gap - gap_mean) * mask
    here = near_scalars(scalars)
    near1 = near1 + (here[:, 1:2] - gap_mean) * mask_near
    projs1 = proj_rows(proj_in.at[1]) + (scalars[:, 1:2] - gap_mean) * mask_projs
    image = operate(direction, near1, projs1)

    image_sum = total(mask * image)
    image_centre = image_sum / safe_count
    centred = (image - image_centre) * mask
    norm_own = total(direction * direction)
    direction_sum = total(mask * direction)
    cross = total(mask * image * direction)
    fit = (cross - image_centre * direction_sum) / jnp.where(norm_own > 0.0, norm_own, 1.0)
    local = centred - fit * direction
    send_field(2, local)
    first = project_fine(local)
    small = centred * SCALE
    send_proj(
        proj_out.at[2],
        proj_in.at[2],
        3,
        (
            first[:, :128],
            first[:, 128:],
            scalar_row(
                image_sum,
                cross,
                direction_sum,
                norm_own,
                total(small * small),
                image_centre,
                fit,
            ),
        ),
    )

    field_here(2)
    near2 = near_products(gather_field(2))
    proj_all(proj_in.at[2], 3).wait_recv()
    scalars = rows_of(proj_in.at[2], 2)
    sums = jnp.sum(scalars, axis=0, keepdims=True)
    image_mean = sums[:, 0:1] / count
    norm_old = sums[:, 3:4]
    step = norm_old / (sums[:, 1:2] - image_mean * sums[:, 2:3])
    shifts = scalars[:, 5:6] - image_mean
    small_shifts = shifts * SCALE
    spread_sum = sums[:, 4:5] + jnp.sum(
        counts * (small_shifts * small_shifts), axis=0, keepdims=True
    )
    long_step = step / SCALE
    norm_now = long_step * (long_step * spread_sum) - norm_old
    ratio = norm_now / norm_old
    pressure = pressure - step * direction
    gap = gap - step * image
    shifted = (gap - (gap_mean - step * image_mean)) * mask
    previous = direction
    direction = shifted + ratio * previous
    here = near_scalars(scalars)
    near2 = (
        (1.0 + ratio - step * here[:, 6:7]) * near1
        - step * near2
        - step * (here[:, 5:6] - image_mean) * mask_near
    )
    projs2 = (
        (1.0 + ratio - step * scalars[:, 6:7]) * projs1
        - step * proj_rows(proj_in.at[2])
        - step * shifts * mask_projs
    )
    image = operate(direction, near2, projs2)

    for ref, value in (
        (pressure_out, pressure),
        (gap_out, gap),
        (direction_out, direction),
        (image_out, image),
    ):
        ref[pl.ds(0, CL, stride=2), :] = value[:, :128]
        ref[pl.ds(1, CL, stride=2), :] = value[:, 128:]

    send_proj(
        last_out,
        last_in,
        4,
        (
            scalar_row(
                total(mask * image),
                total(mask * image * direction),
                total(mask * direction),
                total(shifted * direction),
            ),
        ),
    )
    proj_all(last_in, 4).wait_recv()
    sums = jnp.sum(last_in[...], axis=0, keepdims=True)
    image_mean = sums[:, 0:1] / count
    step = sums[:, 3:4] / (sums[:, 1:2] - image_mean * sums[:, 2:3])
    step_out[...] = jnp.broadcast_to(step, step_out.shape)

    for phase in range(3):
        for kind in range(3):
            field_all(phase, kind).wait_send()
    proj_all(proj0_in, 0).wait_send()
    for i in range(3):
        proj_all(proj_in.at[i], i + 1).wait_send()
    proj_all(last_in, 4).wait_send()


def shards(
    pressure_init,
    gap_height,
    active,
    self_compliance,
    near_blocks,
    near_list,
    far_list,
    source_basis,
    target_basis,
    coupling,
):
    elements = pressure_init.shape[0]
    fold_shape = (elements // 128, 128)
    vmem = pltpu.VMEM
    scratch = [
        vmem(fold_shape, F32),
        vmem(fold_shape, F32),
        vmem(fold_shape, jnp.int32),
        vmem(fold_shape, F32),
        vmem((CL, NEAR, CS, CS), BF16),
        vmem((CL, NEAR), jnp.int32),
        vmem((CL, FAR), jnp.int32),
        vmem((CL * RANK, CS), BF16),
        vmem((CL * RANK, CS), BF16),
        vmem((FAR, CL, RANK * RANK), BF16),
        vmem((2 * NEAR * CL, WINDOW * 2 * CL), BF16),
        vmem((NEAR * CL, DEVICES), BF16),
        vmem((FAR * CL, DEVICES), BF16),
        vmem((FAR * CL, CS), F32),
        vmem((CS, RANK * RANK), BF16),
        vmem((RANK * RANK, CS), BF16),
        vmem((NEAR * CL, CS), F32),
        vmem((3, 1, 2 * CL, 128), BF16),
        vmem((3, WINDOW, 2 * CL, 128), BF16),
        vmem((2, 128), F32),
        vmem((DEVICES * 2, 128), F32),
        vmem((3, 3, 128), F32),
        vmem((3, DEVICES * 3, 128), F32),
        vmem((1, 128), F32),
        vmem((DEVICES, 128), F32),
        pltpu.SemaphoreType.DMA((10,)),
        pltpu.SemaphoreType.DMA((3, 3)),
        pltpu.SemaphoreType.DMA((3, 3)),
        pltpu.SemaphoreType.DMA((5,)),
        pltpu.SemaphoreType.DMA((5,)),
    ]
    pressure, gap, direction, image, step = pl.pallas_call(
        kernel,
        out_shape=[jax.ShapeDtypeStruct(fold_shape, F32)] * 5,
        in_specs=[pl.BlockSpec(memory_space=pl.ANY)] * 10,
        out_specs=[pl.BlockSpec(memory_space=pltpu.VMEM)] * 5,
        scratch_shapes=scratch,
        compiler_params=pltpu.CompilerParams(
            collective_id=0, has_side_effects=True, vmem_limit_bytes=60 * 2**20
        ),
    )(
        pressure_init.reshape(fold_shape),
        gap_height.reshape(fold_shape),
        active.reshape(fold_shape),
        self_compliance.reshape(fold_shape),
        near_blocks,
        near_list,
        far_list,
        source_basis.reshape(CL * RANK, CS),
        target_basis.reshape(CL * RANK, CS),
        jnp.transpose(coupling, (1, 0, 2)),
    )
    pressure = pressure - step * direction
    gap = gap - step * image
    return pressure.reshape(elements), gap.reshape(elements)


def solution(mesh):
    spec = P(("group", "member"))
    return jax.shard_map(
        shards, mesh=mesh, in_specs=(spec,) * 10, out_specs=(spec, spec), check_vma=False
    )
```

```python
import functools

import jax
import jax.numpy as jnp
from jax import lax
from jax.experimental import pallas as pl
from jax.experimental.pallas import tpu as pltpu
from jax.sharding import PartitionSpec as P

MESH = pl.DeviceIdType.MESH
F32 = jnp.float32
BF16 = jnp.bfloat16
GROUPS = 8
MEMBERS = 16
DEVICES = GROUPS * MEMBERS
CL = 8
CS = 256
RANK = 32
NEAR = 9
FAR = 27
WINDOW = 3 * MEMBERS
SCALE = 2.0**-20


def hops(slot):
    steps = (slot & 3, slot >> 2 & 3, slot >> 5)
    return sum(min(step, 4 - step) for step in steps)


FAR_FIRST = sorted(range(1, DEVICES), key=lambda slot: -hops(slot))
FIELD_FIRST = sorted(range(MEMBERS), key=lambda slot: -hops(slot))


def dot(a, b, dims=((1,), (0,))):
    return lax.dot_general(a, b, (dims, ((), ())), preferred_element_type=F32)


def split3(a):
    hi = a.astype(BF16)
    rest = a - hi.astype(F32)
    mid = rest.astype(BF16)
    low = (rest - mid.astype(F32)).astype(BF16)
    return hi, mid, low


def total(a):
    return jnp.sum(jnp.sum(a, axis=0, keepdims=True), axis=1, keepdims=True)


def kernel(
    pressure_hbm,
    height_hbm,
    active_hbm,
    self_hbm,
    near_hbm,
    near_list_hbm,
    far_list_hbm,
    source_hbm,
    target_hbm,
    coupling_hbm,
    pressure_out,
    gap_out,
    direction_out,
    image_out,
    step_out,
    pressure_v,
    height_v,
    active_v,
    self_v,
    near_v,
    near_list_v,
    far_list_v,
    source_v,
    target_v,
    coupling_v,
    near_pick,
    near_dev,
    far_pick,
    far_seg,
    spread,
    fold,
    rows_v,
    field_out,
    field_in,
    proj0_out,
    proj0_in,
    proj_out,
    proj_in,
    last_out,
    last_in,
    load_sem,
    field_send,
    field_recv,
    proj_send,
    proj_recv,
):
    g = lax.axis_index("group")
    m = lax.axis_index("member")

    def around(dy, dz):
        return lax.bitwise_and(m + 4 * dy, 12) + lax.bitwise_and(m + dz, 3)

    groups = [lax.bitwise_and(g + 2 * dx, 6) + lax.bitwise_xor(lax.bitwise_and(g, 1), dc) for dx in range(4) for dc in range(2)]
    members = [around(dy, dz) for dy in range(4) for dz in range(4)]

    def peer(slot):
        return groups[slot // MEMBERS], members[slot % MEMBERS]

    barrier = pltpu.get_barrier_semaphore()

    for slot in FAR_FIRST:
        pl.semaphore_signal(barrier, inc=1, device_id=peer(slot), device_id_type=MESH)

    pairs = (
        (pressure_hbm, pressure_v),
        (active_hbm, active_v),
        (source_hbm, source_v),
        (near_list_hbm, near_list_v),
        (far_list_hbm, far_list_v),
        (self_hbm, self_v),
        (height_hbm, height_v),
        (coupling_hbm, coupling_v),
        (target_hbm, target_v),
        (near_hbm, near_v),
    )
    loads = [pltpu.make_async_copy(a, b, load_sem.at[i]) for i, (a, b) in enumerate(pairs)]
    for load in loads:
        load.start()

    def wide(ref):
        return jnp.concatenate(
            [ref[pl.ds(0, CL, stride=2), :], ref[pl.ds(1, CL, stride=2), :]], axis=1
        )

    def tall(value):
        return jnp.concatenate([value[:, :128], value[:, 128:]], axis=0)

    row8 = lax.broadcasted_iota(jnp.int32, (CL, CS), 0)
    lane8 = lax.broadcasted_iota(jnp.int32, (CL, CS), 1)
    own = row8 == lax.shift_right_logical(lane8, 5)

    def project(value16):
        product = dot(value16, source_v[...], ((1,), (1,)))
        first = jnp.sum(jnp.where(own, product[:CL], 0.0), axis=0, keepdims=True)
        second = jnp.sum(jnp.where(own, product[CL:], 0.0), axis=0, keepdims=True)
        return first, second

    def project_fine(value):
        product = dot(jnp.concatenate(split3(value), axis=0), source_v[...], ((1,), (1,)))
        product = product[:CL] + (product[CL : 2 * CL] + product[2 * CL :])
        return jnp.sum(jnp.where(own, product, 0.0), axis=0, keepdims=True)

    lane1 = lax.broadcasted_iota(jnp.int32, (1, 128), 1)

    def scalar_row(*values):
        row = jnp.zeros((1, 128), F32)
        for i, value in enumerate(values):
            row = jnp.where(lane1 == i, value, row)
        return row

    odd = lax.bitwise_and(g, 1)
    partner = lax.bitwise_xor(g, 1)
    across = lax.bitwise_and(g - 1 + 2 * odd, 7)

    def field_copy(phase, kind, src, start, to, count=1):
        return pltpu.make_async_remote_copy(
            src_ref=src,
            dst_ref=field_in.at[phase, pl.ds(start, count)],
            send_sem=field_send.at[phase, kind],
            recv_sem=field_recv.at[phase, kind],
            device_id=to,
            device_id_type=MESH,
        )

    def field_all(phase, kind):
        start, count = ((1, MEMBERS - 1), (MEMBERS, MEMBERS), (2 * MEMBERS, MEMBERS))[kind]
        rest = field_in.at[phase, pl.ds(start, count)]
        return field_copy(phase, kind, rest, start, peer(1), count)

    def forward(phase):
        field_all(phase, 0).wait_recv()
        whole = field_in.at[phase, pl.ds(0, MEMBERS)]
        field_copy(phase, 2, whole, (1 + odd) * MEMBERS, (partner, m), MEMBERS).start()

    def field_here(phase):
        forward(phase)
        field_all(phase, 1).wait_recv()
        field_all(phase, 2).wait_recv()

    def proj_copy(out, into, sem, slot):
        return pltpu.make_async_remote_copy(
            src_ref=out,
            dst_ref=into.at[pl.ds(slot * out.shape[0], out.shape[0])],
            send_sem=proj_send.at[sem],
            recv_sem=proj_recv.at[sem],
            device_id=peer(slot),
            device_id_type=MESH,
        )

    def proj_all(into, sem):
        each = into.shape[0] // DEVICES
        rest = into.at[pl.ds(each, (DEVICES - 1) * each)]
        return pltpu.make_async_remote_copy(
            src_ref=rest,
            dst_ref=rest,
            send_sem=proj_send.at[sem],
            recv_sem=proj_recv.at[sem],
            device_id=peer(1),
            device_id_type=MESH,
        )

    def send_field(phase, value):
        block = tall(value).astype(BF16)
        field_out[phase, 0] = block
        field_in[phase, 0] = block
        src = field_out.at[phase]
        for slot in FIELD_FIRST:
            if slot:
                field_copy(phase, 0, src, slot, (g, members[slot])).start()
        for slot in FIELD_FIRST:
            field_copy(phase, 1, src, (2 - odd) * MEMBERS + slot, (across, members[slot])).start()

    def send_proj(out, into, sem, rows):
        for i, row in enumerate(rows):
            out[i : i + 1, :] = row
            into[i : i + 1, :] = row
        for slot in FAR_FIRST:
            proj_copy(out, into, sem, slot).start()

    loads[0].wait()
    loads[1].wait()
    mask = wide(active_v).astype(F32)
    pressure = wide(pressure_v) * mask
    loads[2].wait()
    first, mask_proj = project(jnp.concatenate([pressure, mask], axis=0).astype(BF16))
    count_own = total(mask)

    loads[3].wait()
    loads[4].wait()
    near_ids = near_list_v[...]

    def member_part(ids):
        dy = lax.bitwise_and(m - lax.bitwise_and(lax.shift_right_logical(ids, 3), 12), 12)
        return dy + lax.bitwise_and(m - lax.shift_right_logical(ids, 3), 3)

    def group_part(ids):
        theirs = lax.shift_right_logical(ids, 7)
        dx = lax.bitwise_and(g - lax.bitwise_and(theirs, 6), 6)
        return (dx + lax.bitwise_and(g + theirs, 1)) * MEMBERS

    dg = lax.bitwise_and(g - lax.shift_right_logical(near_ids, 7), 7)
    near_slot = jnp.where(dg == 7, 2, dg) * MEMBERS + member_part(near_ids)
    near_row = near_slot * (2 * CL) + lax.bitwise_and(near_ids, 7)
    dev_row = group_part(near_ids) + member_part(near_ids)
    pick_iota = lax.broadcasted_iota(jnp.int32, (CL, WINDOW * 2 * CL), 1)
    dev_iota = lax.broadcasted_iota(jnp.int32, (CL, DEVICES), 1)
    low, high, dev = [], [], []
    for n in range(NEAR):
        low.append(jnp.where(pick_iota == near_row[:, n : n + 1], 1.0, 0.0))
        high.append(jnp.where(pick_iota == near_row[:, n : n + 1] + CL, 1.0, 0.0))
        dev.append(jnp.where(dev_iota == dev_row[:, n : n + 1], 1.0, 0.0))
    near_pick[...] = jnp.concatenate(low + high, axis=0).astype(BF16)
    near_dev[...] = jnp.concatenate(dev, axis=0).astype(BF16)

    far_ids = far_list_v[...]
    far_row = group_part(far_ids) + member_part(far_ids)
    far_part = lax.bitwise_and(far_ids, 7)
    part_iota = lax.shift_right_logical(lane8, 5)
    picks, parts = [], []
    for f in range(FAR):
        picks.append(jnp.where(dev_iota == far_row[:, f : f + 1], 1.0, 0.0))
        parts.append(jnp.where(part_iota == far_part[:, f : f + 1], 1.0, 0.0))
    far_pick[...] = jnp.concatenate(picks, axis=0).astype(BF16)
    far_seg[...] = jnp.concatenate(parts, axis=0)
    tall_iota = lax.bitwise_and(lax.broadcasted_iota(jnp.int32, (CS, RANK * RANK), 0), RANK - 1)
    wide_iota = lax.bitwise_and(lax.broadcasted_iota(jnp.int32, (CS, RANK * RANK), 1), RANK - 1)
    spread[...] = jnp.where(tall_iota == wide_iota, 1.0, 0.0).astype(BF16)
    tall_iota = lax.shift_right_logical(lax.broadcasted_iota(jnp.int32, (RANK * RANK, CS), 0), 5)
    wide_iota = lax.bitwise_and(lax.broadcasted_iota(jnp.int32, (RANK * RANK, CS), 1), RANK - 1)
    fold[...] = jnp.where(tall_iota == wide_iota, 1.0, 0.0).astype(BF16)
    pl.semaphore_wait(barrier, DEVICES - 1)
    send_field(0, pressure)
    send_proj(proj0_out, proj0_in, 0, (first[:, :128], first[:, 128:]))

    for load in loads[5:]:
        load.wait()
    compliance = wide(self_v)
    height = wide(height_v)

    def turn(c, carry):
        for n in range(NEAR):
            near_v[c, n] = jnp.transpose(near_v[c, n])
        return carry

    lax.fori_loop(0, CL, turn, 0)

    row16 = lax.broadcasted_iota(jnp.int32, (2 * CL, CS), 0)

    def gather_field(phase):
        window = field_in[phase].reshape(WINDOW * 2 * CL, 128)
        picked = dot(near_pick[...], window)
        half = NEAR * CL
        return jnp.concatenate([picked[:half], picked[half:]], axis=1)

    def near_products(rows):
        rows_v[...] = rows
        products = []
        for n in range(NEAR):
            acc = jnp.zeros((2 * CL, CS), F32)
            for c in range(CL):
                row = rows_v[n * CL + c : n * CL + c + 1, :]
                left = jnp.where(row16 == c, row, 0.0).astype(BF16)
                acc = acc + dot(left, near_v[c, n])
            products.append(acc[:CL])
        return jnp.concatenate(products, axis=0)

    def slot_sum(products):
        out = products[:CL]
        for n in range(1, NEAR):
            out = out + products[n * CL : (n + 1) * CL]
        return out

    def far_sum(projected):
        picked = dot(far_pick[...], projected.astype(BF16))
        spreaded = dot((picked * far_seg[...]).astype(BF16), spread[...])
        summed = jnp.zeros((CL, RANK * RANK), F32)
        for f in range(FAR):
            summed = summed + spreaded[f * CL : (f + 1) * CL] * coupling_v[f].astype(F32)
        high = summed.astype(BF16).astype(F32)
        both = dot(jnp.concatenate([high, summed - high], axis=0).astype(BF16), fold[...])
        coupled = both[:CL] + both[CL:]
        return dot(jnp.where(own, coupled, 0.0).astype(BF16), target_v[...])

    def operate(value, products, projected):
        narrow = value.astype(BF16).astype(F32)
        return compliance * narrow + (slot_sum(products) + far_sum(projected))

    def rows_of(ref, i):
        return ref[pl.ds(i, DEVICES, stride=ref.shape[0] // DEVICES), :]

    def proj_rows(ref):
        return jnp.concatenate([rows_of(ref, 0), rows_of(ref, 1)], axis=1)

    def near_scalars(scalars):
        picked = dot(near_dev[...], jnp.concatenate(split3(scalars), axis=1))
        return picked[:, :128] + (picked[:, 128:256] + picked[:, 256:])

    field_here(0)
    rows0 = gather_field(0)
    mask_rows = jnp.where(rows0 != 0.0, 1.0, 0.0)
    send_proj(
        proj_out.at[0],
        proj_in.at[0],
        1,
        (mask_proj[:, :128], mask_proj[:, 128:], scalar_row(count_own)),
    )
    near0 = near_products(rows0)
    proj_all(proj0_in, 0).wait_recv()
    gap = operate(pressure, near0, proj_rows(proj0_in)) - height

    safe_count = jnp.maximum(count_own, 1.0)
    first = project_fine(mask * gap)
    gap_sum = total(mask * gap)
    gap_centre = gap_sum / safe_count
    local = (gap - gap_centre) * mask
    send_field(1, local)
    send_proj(
        proj_out.at[1],
        proj_in.at[1],
        2,
        (first[:, :128], first[:, 128:], scalar_row(gap_sum, gap_centre)),
    )

    mask_near = near_products(mask_rows)
    proj_all(proj_in.at[0], 1).wait_recv()
    mask_projs = proj_rows(proj_in.at[0])
    counts = rows_of(proj_in.at[0], 2)[:, 0:1]
    count = jnp.sum(counts, axis=0, keepdims=True)

    field_here(1)
    near1 = near_products(gather_field(1))
    proj_all(proj_in.at[1], 2).wait_recv()
    scalars = rows_of(proj_in.at[1], 2)
    gap_mean = jnp.sum(scalars[:, 0:1], axis=0, keepdims=True) / count
    direction = (gap - gap_mean) * mask
    here = near_scalars(scalars)
    near1 = near1 + (here[:, 1:2] - gap_mean) * mask_near
    projs1 = proj_rows(proj_in.at[1]) - gap_mean * mask_projs
    image = operate(direction, near1, projs1)

    first = project_fine(mask * image)
    image_sum = total(mask * image)
    image_centre = image_sum / safe_count
    centred = (image - image_centre) * mask
    norm_own = total(direction * direction)
    direction_sum = total(mask * direction)
    cross = total(mask * image * direction)
    fit = (cross - image_centre * direction_sum) / jnp.where(norm_own > 0.0, norm_own, 1.0)
    local = centred - fit * direction
    send_field(2, local)
    small = centred * SCALE
    send_proj(
        proj_out.at[2],
        proj_in.at[2],
        3,
        (
            first[:, :128],
            first[:, 128:],
            scalar_row(
                image_sum,
                cross,
                direction_sum,
                norm_own,
                total(small * small),
                image_centre,
                fit,
            ),
        ),
    )

    field_here(2)
    near2 = near_products(gather_field(2))
    proj_all(proj_in.at[2], 3).wait_recv()
    scalars = rows_of(proj_in.at[2], 2)
    sums = jnp.sum(scalars, axis=0, keepdims=True)
    image_mean = sums[:, 0:1] / count
    norm_old = sums[:, 3:4]
    step = norm_old / (sums[:, 1:2] - image_mean * sums[:, 2:3])
    shifts = scalars[:, 5:6] - image_mean
    small_shifts = shifts * SCALE
    spread_sum = sums[:, 4:5] + jnp.sum(
        counts * (small_shifts * small_shifts), axis=0, keepdims=True
    )
    long_step = step / SCALE
    norm_now = long_step * (long_step * spread_sum) - norm_old
    ratio = norm_now / norm_old
    pressure = pressure - step * direction
    gap = gap - step * image
    shifted = (gap - (gap_mean - step * image_mean)) * mask
    previous = direction
    direction = shifted + ratio * previous
    here = near_scalars(scalars)
    near2 = (
        (1.0 + ratio - step * here[:, 6:7]) * near1
        - step * near2
        - step * (here[:, 5:6] - image_mean) * mask_near
    )
    projs2 = (1.0 + ratio) * projs1 - step * (
        proj_rows(proj_in.at[2]) - image_mean * mask_projs
    )
    image = operate(direction, near2, projs2)

    for ref, value in (
        (pressure_out, pressure),
        (gap_out, gap),
        (direction_out, direction),
        (image_out, image),
    ):
        ref[pl.ds(0, CL, stride=2), :] = value[:, :128]
        ref[pl.ds(1, CL, stride=2), :] = value[:, 128:]

    send_proj(
        last_out,
        last_in,
        4,
        (
            scalar_row(
                total(mask * image),
                total(mask * image * direction),
                total(mask * direction),
                total(shifted * direction),
            ),
        ),
    )
    proj_all(last_in, 4).wait_recv()
    sums = jnp.sum(last_in[...], axis=0, keepdims=True)
    image_mean = sums[:, 0:1] / count
    step = sums[:, 3:4] / (sums[:, 1:2] - image_mean * sums[:, 2:3])
    step_out[...] = jnp.broadcast_to(step, step_out.shape)

    for phase in range(3):
        for kind in range(3):
            field_all(phase, kind).wait_send()
    proj_all(proj0_in, 0).wait_send()
    for i in range(3):
        proj_all(proj_in.at[i], i + 1).wait_send()
    proj_all(last_in, 4).wait_send()


def shards(
    pressure_init,
    gap_height,
    active,
    self_compliance,
    near_blocks,
    near_list,
    far_list,
    source_basis,
    target_basis,
    coupling,
):
    elements = pressure_init.shape[0]
    fold_shape = (elements // 128, 128)
    vmem = pltpu.VMEM
    scratch = [
        vmem(fold_shape, F32),
        vmem(fold_shape, F32),
        vmem(fold_shape, jnp.int32),
        vmem(fold_shape, F32),
        vmem((CL, NEAR, CS, CS), BF16),
        vmem((CL, NEAR), jnp.int32),
        vmem((CL, FAR), jnp.int32),
        vmem((CL * RANK, CS), BF16),
        vmem((CL * RANK, CS), BF16),
        vmem((FAR, CL, RANK * RANK), BF16),
        vmem((2 * NEAR * CL, WINDOW * 2 * CL), BF16),
        vmem((NEAR * CL, DEVICES), BF16),
        vmem((FAR * CL, DEVICES), BF16),
        vmem((FAR * CL, CS), F32),
        vmem((CS, RANK * RANK), BF16),
        vmem((RANK * RANK, CS), BF16),
        vmem((NEAR * CL, CS), F32),
        vmem((3, 1, 2 * CL, 128), BF16),
        vmem((3, WINDOW, 2 * CL, 128), BF16),
        vmem((2, 128), F32),
        vmem((DEVICES * 2, 128), F32),
        vmem((3, 3, 128), F32),
        vmem((3, DEVICES * 3, 128), F32),
        vmem((1, 128), F32),
        vmem((DEVICES, 128), F32),
        pltpu.SemaphoreType.DMA((10,)),
        pltpu.SemaphoreType.DMA((3, 3)),
        pltpu.SemaphoreType.DMA((3, 3)),
        pltpu.SemaphoreType.DMA((5,)),
        pltpu.SemaphoreType.DMA((5,)),
    ]
    pressure, gap, direction, image, step = pl.pallas_call(
        kernel,
        out_shape=[jax.ShapeDtypeStruct(fold_shape, F32)] * 5,
        in_specs=[pl.BlockSpec(memory_space=pl.ANY)] * 10,
        out_specs=[pl.BlockSpec(memory_space=pltpu.VMEM)] * 5,
        scratch_shapes=scratch,
        compiler_params=pltpu.CompilerParams(
            collective_id=0, has_side_effects=True, vmem_limit_bytes=60 * 2**20
        ),
    )(
        pressure_init.reshape(fold_shape),
        gap_height.reshape(fold_shape),
        active.reshape(fold_shape),
        self_compliance.reshape(fold_shape),
        near_blocks,
        near_list,
        far_list,
        source_basis.reshape(CL * RANK, CS),
        target_basis.reshape(CL * RANK, CS),
        jnp.transpose(coupling, (1, 0, 2)),
    )
    pressure = pressure - step * direction
    gap = gap - step * image
    return pressure.reshape(elements), gap.reshape(elements)


def solution(mesh):
    spec = P(("group", "member"))
    return jax.shard_map(
        shards, mesh=mesh, in_specs=(spec,) * 10, out_specs=(spec, spec), check_vma=False
    )
```

```python
import functools

import jax
import jax.numpy as jnp
from jax import lax
from jax.experimental import pallas as pl
from jax.experimental.pallas import tpu as pltpu
from jax.sharding import PartitionSpec as P

MESH = pl.DeviceIdType.MESH
F32 = jnp.float32
BF16 = jnp.bfloat16
GROUPS = 8
MEMBERS = 16
DEVICES = GROUPS * MEMBERS
CL = 8
CS = 256
RANK = 32
NEAR = 9
FAR = 27
WINDOW = 3 * MEMBERS
SCALE = 2.0**-20


def hops(slot):
    steps = (slot & 3, slot >> 2 & 3, slot >> 5)
    return sum(min(step, 4 - step) for step in steps)


FAR_FIRST = sorted(range(1, DEVICES), key=lambda slot: -hops(slot))
FIELD_FIRST = sorted(range(MEMBERS), key=lambda slot: -hops(slot))


def dot(a, b, dims=((1,), (0,))):
    return lax.dot_general(a, b, (dims, ((), ())), preferred_element_type=F32)


def split3(a):
    hi = a.astype(BF16)
    rest = a - hi.astype(F32)
    mid = rest.astype(BF16)
    low = (rest - mid.astype(F32)).astype(BF16)
    return hi, mid, low


def total(a):
    return jnp.sum(jnp.sum(a, axis=0, keepdims=True), axis=1, keepdims=True)


def kernel(
    pressure_hbm,
    height_hbm,
    active_hbm,
    self_hbm,
    near_hbm,
    near_list_hbm,
    far_list_hbm,
    source_hbm,
    target_hbm,
    coupling_hbm,
    pressure_out,
    gap_out,
    direction_out,
    image_out,
    step_out,
    pressure_v,
    height_v,
    active_v,
    self_v,
    near_v,
    near_list_v,
    far_list_v,
    source_v,
    target_v,
    coupling_v,
    near_pick,
    near_dev,
    far_pick,
    far_seg,
    spread,
    fold,
    rows_v,
    field_out,
    field_in,
    proj0_out,
    proj0_in,
    proj_out,
    proj_in,
    last_out,
    last_in,
    load_sem,
    field_send,
    field_recv,
    proj_send,
    proj_recv,
):
    g = lax.axis_index("group")
    m = lax.axis_index("member")

    def around(dy, dz):
        return lax.bitwise_and(m + 4 * dy, 12) + lax.bitwise_and(m + dz, 3)

    groups = [lax.bitwise_and(g + 2 * dx, 6) + lax.bitwise_xor(lax.bitwise_and(g, 1), dc) for dx in range(4) for dc in range(2)]
    members = [around(dy, dz) for dy in range(4) for dz in range(4)]

    def peer(slot):
        return groups[slot // MEMBERS], members[slot % MEMBERS]

    barrier = pltpu.get_barrier_semaphore()

    for slot in FAR_FIRST:
        pl.semaphore_signal(barrier, inc=1, device_id=peer(slot), device_id_type=MESH)

    pairs = (
        (pressure_hbm, pressure_v),
        (active_hbm, active_v),
        (source_hbm, source_v),
        (near_list_hbm, near_list_v),
        (far_list_hbm, far_list_v),
        (self_hbm, self_v),
        (height_hbm, height_v),
        (coupling_hbm, coupling_v),
        (target_hbm, target_v),
        (near_hbm, near_v),
    )
    loads = [pltpu.make_async_copy(a, b, load_sem.at[i]) for i, (a, b) in enumerate(pairs)]
    for load in loads:
        load.start()

    def wide(ref):
        return jnp.concatenate(
            [ref[pl.ds(0, CL, stride=2), :], ref[pl.ds(1, CL, stride=2), :]], axis=1
        )

    def tall(value):
        return jnp.concatenate([value[:, :128], value[:, 128:]], axis=0)

    row8 = lax.broadcasted_iota(jnp.int32, (CL, CS), 0)
    lane8 = lax.broadcasted_iota(jnp.int32, (CL, CS), 1)
    own = row8 == lax.shift_right_logical(lane8, 5)

    def project(value16):
        product = dot(value16, source_v[...], ((1,), (1,)))
        first = jnp.sum(jnp.where(own, product[:CL], 0.0), axis=0, keepdims=True)
        second = jnp.sum(jnp.where(own, product[CL:], 0.0), axis=0, keepdims=True)
        return first, second

    def project_fine(value):
        product = dot(jnp.concatenate(split3(value), axis=0), source_v[...], ((1,), (1,)))
        product = product[:CL] + (product[CL : 2 * CL] + product[2 * CL :])
        return jnp.sum(jnp.where(own, product, 0.0), axis=0, keepdims=True)

    lane1 = lax.broadcasted_iota(jnp.int32, (1, 128), 1)

    def scalar_row(*values):
        row = jnp.zeros((1, 128), F32)
        for i, value in enumerate(values):
            row = jnp.where(lane1 == i, value, row)
        return row

    odd = lax.bitwise_and(g, 1)
    partner = lax.bitwise_xor(g, 1)
    across = lax.bitwise_and(g - 1 + 2 * odd, 7)

    def field_copy(phase, kind, src, start, to, count=1):
        return pltpu.make_async_remote_copy(
            src_ref=src,
            dst_ref=field_in.at[phase, pl.ds(start, count)],
            send_sem=field_send.at[phase, kind],
            recv_sem=field_recv.at[phase, kind],
            device_id=to,
            device_id_type=MESH,
        )

    def field_all(phase, kind):
        start, count = ((1, MEMBERS - 1), (MEMBERS, MEMBERS), (2 * MEMBERS, MEMBERS))[kind]
        rest = field_in.at[phase, pl.ds(start, count)]
        return field_copy(phase, kind, rest, start, peer(1), count)

    def forward(phase):
        field_all(phase, 0).wait_recv()
        whole = field_in.at[phase, pl.ds(0, MEMBERS)]
        field_copy(phase, 2, whole, (1 + odd) * MEMBERS, (partner, m), MEMBERS).start()

    def field_here(phase):
        forward(phase)
        field_all(phase, 1).wait_recv()
        field_all(phase, 2).wait_recv()

    def proj_copy(out, into, sem, slot):
        return pltpu.make_async_remote_copy(
            src_ref=out,
            dst_ref=into.at[pl.ds(slot * out.shape[0], out.shape[0])],
            send_sem=proj_send.at[sem],
            recv_sem=proj_recv.at[sem],
            device_id=peer(slot),
            device_id_type=MESH,
        )

    def proj_all(into, sem):
        each = into.shape[0] // DEVICES
        rest = into.at[pl.ds(each, (DEVICES - 1) * each)]
        return pltpu.make_async_remote_copy(
            src_ref=rest,
            dst_ref=rest,
            send_sem=proj_send.at[sem],
            recv_sem=proj_recv.at[sem],
            device_id=peer(1),
            device_id_type=MESH,
        )

    def send_field(phase, value):
        block = tall(value).astype(BF16)
        field_out[phase, 0] = block
        field_in[phase, 0] = block
        src = field_out.at[phase]
        for slot in FIELD_FIRST:
            if slot:
                field_copy(phase, 0, src, slot, (g, members[slot])).start()
        for slot in FIELD_FIRST:
            field_copy(phase, 1, src, (2 - odd) * MEMBERS + slot, (across, members[slot])).start()

    def send_proj(out, into, sem, rows):
        for i, row in enumerate(rows):
            out[i : i + 1, :] = row
            into[i : i + 1, :] = row
        for slot in FAR_FIRST:
            proj_copy(out, into, sem, slot).start()

    loads[0].wait()
    loads[1].wait()
    mask = wide(active_v).astype(F32)
    pressure = wide(pressure_v) * mask
    loads[2].wait()
    first, mask_proj = project(jnp.concatenate([pressure, mask], axis=0).astype(BF16))
    count_own = total(mask)

    loads[3].wait()
    loads[4].wait()
    near_ids = near_list_v[...]

    def member_part(ids):
        dy = lax.bitwise_and(m - lax.bitwise_and(lax.shift_right_logical(ids, 3), 12), 12)
        return dy + lax.bitwise_and(m - lax.shift_right_logical(ids, 3), 3)

    def group_part(ids):
        theirs = lax.shift_right_logical(ids, 7)
        dx = lax.bitwise_and(g - lax.bitwise_and(theirs, 6), 6)
        return (dx + lax.bitwise_and(g + theirs, 1)) * MEMBERS

    dg = lax.bitwise_and(g - lax.shift_right_logical(near_ids, 7), 7)
    near_slot = jnp.where(dg == 7, 2, dg) * MEMBERS + member_part(near_ids)
    near_row = near_slot * (2 * CL) + lax.bitwise_and(near_ids, 7)
    dev_row = group_part(near_ids) + member_part(near_ids)
    pick_iota = lax.broadcasted_iota(jnp.int32, (CL, WINDOW * 2 * CL), 1)
    dev_iota = lax.broadcasted_iota(jnp.int32, (CL, DEVICES), 1)
    low, high, dev = [], [], []
    for n in range(NEAR):
        low.append(jnp.where(pick_iota == near_row[:, n : n + 1], 1.0, 0.0))
        high.append(jnp.where(pick_iota == near_row[:, n : n + 1] + CL, 1.0, 0.0))
        dev.append(jnp.where(dev_iota == dev_row[:, n : n + 1], 1.0, 0.0))
    near_pick[...] = jnp.concatenate(low + high, axis=0).astype(BF16)
    near_dev[...] = jnp.concatenate(dev, axis=0).astype(BF16)

    far_ids = far_list_v[...]
    far_row = group_part(far_ids) + member_part(far_ids)
    far_part = lax.bitwise_and(far_ids, 7)
    part_iota = lax.shift_right_logical(lane8, 5)
    picks, parts = [], []
    for f in range(FAR):
        picks.append(jnp.where(dev_iota == far_row[:, f : f + 1], 1.0, 0.0))
        parts.append(jnp.where(part_iota == far_part[:, f : f + 1], 1.0, 0.0))
    far_pick[...] = jnp.concatenate(picks, axis=0).astype(BF16)
    far_seg[...] = jnp.concatenate(parts, axis=0).astype(BF16)
    tall_iota = lax.bitwise_and(lax.broadcasted_iota(jnp.int32, (CS, RANK * RANK), 0), RANK - 1)
    wide_iota = lax.bitwise_and(lax.broadcasted_iota(jnp.int32, (CS, RANK * RANK), 1), RANK - 1)
    spread[...] = jnp.where(tall_iota == wide_iota, 1.0, 0.0).astype(BF16)
    tall_iota = lax.shift_right_logical(lax.broadcasted_iota(jnp.int32, (RANK * RANK, CS), 0), 5)
    wide_iota = lax.bitwise_and(lax.broadcasted_iota(jnp.int32, (RANK * RANK, CS), 1), RANK - 1)
    fold[...] = jnp.where(tall_iota == wide_iota, 1.0, 0.0).astype(BF16)
    pl.semaphore_wait(barrier, DEVICES - 1)
    send_field(0, pressure)
    send_proj(proj0_out, proj0_in, 0, (first[:, :128], first[:, 128:]))

    for load in loads[5:]:
        load.wait()
    compliance = wide(self_v)
    height = wide(height_v)

    def turn(c, carry):
        for n in range(NEAR):
            near_v[c, n] = jnp.transpose(near_v[c, n])
        return carry

    lax.fori_loop(0, CL, turn, 0)

    row16 = row8

    def gather_field(phase):
        window = field_in[phase].reshape(WINDOW * 2 * CL, 128)
        picked = dot(near_pick[...], window)
        half = NEAR * CL
        return jnp.concatenate([picked[:half], picked[half:]], axis=1)

    def near_products(rows):
        rows_v[...] = rows
        products = []
        for n in range(NEAR):
            acc = jnp.zeros((CL, CS), F32)
            for c in range(CL):
                row = rows_v[n * CL + c : n * CL + c + 1, :]
                left = jnp.where(row16 == c, row, 0.0).astype(BF16)
                acc = acc + dot(left, near_v[c, n])
            products.append(acc[:CL])
        return jnp.concatenate(products, axis=0)

    def slot_sum(products):
        out = products[:CL]
        for n in range(1, NEAR):
            out = out + products[n * CL : (n + 1) * CL]
        return out

    def far_sum(projected):
        picked = dot(far_pick[...], projected.astype(BF16))
        spreaded = dot(picked.astype(BF16) * far_seg[...], spread[...])
        summed = jnp.zeros((CL, RANK * RANK), F32)
        for f in range(FAR):
            summed = summed + spreaded[f * CL : (f + 1) * CL] * coupling_v[f].astype(F32)
        high = summed.astype(BF16).astype(F32)
        both = dot(jnp.concatenate([high, summed - high], axis=0).astype(BF16), fold[...])
        coupled = both[:CL] + both[CL:]
        return dot(jnp.where(own, coupled, 0.0).astype(BF16), target_v[...])

    def operate(value, products, projected):
        narrow = value.astype(BF16).astype(F32)
        return compliance * narrow + (slot_sum(products) + far_sum(projected))

    def rows_of(ref, i):
        return ref[pl.ds(i, DEVICES, stride=ref.shape[0] // DEVICES), :]

    def proj_rows(ref):
        return jnp.concatenate([rows_of(ref, 0), rows_of(ref, 1)], axis=1)

    def near_scalars(scalars):
        picked = dot(near_dev[...], jnp.concatenate(split3(scalars), axis=1))
        return picked[:, :128] + (picked[:, 128:256] + picked[:, 256:])

    field_here(0)
    rows0 = gather_field(0)
    mask_rows = jnp.where(rows0 != 0.0, 1.0, 0.0)
    send_proj(
        proj_out.at[0],
        proj_in.at[0],
        1,
        (mask_proj[:, :128], mask_proj[:, 128:], scalar_row(count_own)),
    )
    near0 = near_products(rows0)
    proj_all(proj0_in, 0).wait_recv()
    gap = operate(pressure, near0, proj_rows(proj0_in)) - height

    safe_count = jnp.maximum(count_own, 1.0)
    first = project_fine(mask * gap)
    gap_sum = total(mask * gap)
    gap_centre = gap_sum / safe_count
    local = (gap - gap_centre) * mask
    send_field(1, local)
    send_proj(
        proj_out.at[1],
        proj_in.at[1],
        2,
        (first[:, :128], first[:, 128:], scalar_row(gap_sum, gap_centre)),
    )

    mask_near = near_products(mask_rows)
    proj_all(proj_in.at[0], 1).wait_recv()
    mask_projs = proj_rows(proj_in.at[0])
    counts = rows_of(proj_in.at[0], 2)[:, 0:1]
    count = jnp.sum(counts, axis=0, keepdims=True)

    field_here(1)
    near1 = near_products(gather_field(1))
    proj_all(proj_in.at[1], 2).wait_recv()
    scalars = rows_of(proj_in.at[1], 2)
    gap_mean = jnp.sum(scalars[:, 0:1], axis=0, keepdims=True) / count
    direction = (gap - gap_mean) * mask
    here = near_scalars(scalars)
    near1 = near1 + (here[:, 1:2] - gap_mean) * mask_near
    projs1 = proj_rows(proj_in.at[1]) - gap_mean * mask_projs
    image = operate(direction, near1, projs1)

    first = project_fine(mask * image)
    image_sum = total(mask * image)
    image_centre = image_sum / safe_count
    centred = (image - image_centre) * mask
    norm_own = total(direction * direction)
    direction_sum = total(mask * direction)
    cross = total(mask * image * direction)
    fit = (cross - image_centre * direction_sum) / jnp.where(norm_own > 0.0, norm_own, 1.0)
    local = centred - fit * direction
    send_field(2, local)
    small = centred * SCALE
    send_proj(
        proj_out.at[2],
        proj_in.at[2],
        3,
        (
            first[:, :128],
            first[:, 128:],
            scalar_row(
                image_sum,
                cross,
                direction_sum,
                norm_own,
                total(small * small),
                image_centre,
                fit,
            ),
        ),
    )

    field_here(2)
    near2 = near_products(gather_field(2))
    proj_all(proj_in.at[2], 3).wait_recv()
    scalars = rows_of(proj_in.at[2], 2)
    sums = jnp.sum(scalars, axis=0, keepdims=True)
    image_mean = sums[:, 0:1] / count
    norm_old = sums[:, 3:4]
    step = norm_old / (sums[:, 1:2] - image_mean * sums[:, 2:3])
    shifts = scalars[:, 5:6] - image_mean
    small_shifts = shifts * SCALE
    spread_sum = sums[:, 4:5] + jnp.sum(
        counts * (small_shifts * small_shifts), axis=0, keepdims=True
    )
    long_step = step / SCALE
    norm_now = long_step * (long_step * spread_sum) - norm_old
    ratio = norm_now / norm_old
    pressure = pressure - step * direction
    gap = gap - step * image
    shifted = (gap - (gap_mean - step * image_mean)) * mask
    previous = direction
    direction = shifted + ratio * previous
    here = near_scalars(scalars)
    near2 = (
        (1.0 + ratio - step * here[:, 6:7]) * near1
        - step * near2
        - step * (here[:, 5:6] - image_mean) * mask_near
    )
    projs2 = (1.0 + ratio) * projs1 - step * (
        proj_rows(proj_in.at[2]) - image_mean * mask_projs
    )
    image = operate(direction, near2, projs2)

    for ref, value in (
        (pressure_out, pressure),
        (gap_out, gap),
        (direction_out, direction),
        (image_out, image),
    ):
        ref[pl.ds(0, CL, stride=2), :] = value[:, :128]
        ref[pl.ds(1, CL, stride=2), :] = value[:, 128:]

    send_proj(
        last_out,
        last_in,
        4,
        (
            scalar_row(
                total(mask * image),
                total(mask * image * direction),
                total(mask * direction),
                total(shifted * direction),
            ),
        ),
    )
    proj_all(last_in, 4).wait_recv()
    sums = jnp.sum(last_in[...], axis=0, keepdims=True)
    image_mean = sums[:, 0:1] / count
    step = sums[:, 3:4] / (sums[:, 1:2] - image_mean * sums[:, 2:3])
    step_out[...] = jnp.broadcast_to(step, step_out.shape)

    for phase in range(3):
        for kind in range(3):
            field_all(phase, kind).wait_send()
    proj_all(proj0_in, 0).wait_send()
    for i in range(3):
        proj_all(proj_in.at[i], i + 1).wait_send()
    proj_all(last_in, 4).wait_send()


def shards(
    pressure_init,
    gap_height,
    active,
    self_compliance,
    near_blocks,
    near_list,
    far_list,
    source_basis,
    target_basis,
    coupling,
):
    elements = pressure_init.shape[0]
    fold_shape = (elements // 128, 128)
    vmem = pltpu.VMEM
    scratch = [
        vmem(fold_shape, F32),
        vmem(fold_shape, F32),
        vmem(fold_shape, jnp.int32),
        vmem(fold_shape, F32),
        vmem((CL, NEAR, CS, CS), BF16),
        vmem((CL, NEAR), jnp.int32),
        vmem((CL, FAR), jnp.int32),
        vmem((CL * RANK, CS), BF16),
        vmem((CL * RANK, CS), BF16),
        vmem((FAR, CL, RANK * RANK), BF16),
        vmem((2 * NEAR * CL, WINDOW * 2 * CL), BF16),
        vmem((NEAR * CL, DEVICES), BF16),
        vmem((FAR * CL, DEVICES), BF16),
        vmem((FAR * CL, CS), BF16),
        vmem((CS, RANK * RANK), BF16),
        vmem((RANK * RANK, CS), BF16),
        vmem((NEAR * CL, CS), F32),
        vmem((3, 1, 2 * CL, 128), BF16),
        vmem((3, WINDOW, 2 * CL, 128), BF16),
        vmem((2, 128), F32),
        vmem((DEVICES * 2, 128), F32),
        vmem((3, 3, 128), F32),
        vmem((3, DEVICES * 3, 128), F32),
        vmem((1, 128), F32),
        vmem((DEVICES, 128), F32),
        pltpu.SemaphoreType.DMA((10,)),
        pltpu.SemaphoreType.DMA((3, 3)),
        pltpu.SemaphoreType.DMA((3, 3)),
        pltpu.SemaphoreType.DMA((5,)),
        pltpu.SemaphoreType.DMA((5,)),
    ]
    pressure, gap, direction, image, step = pl.pallas_call(
        kernel,
        out_shape=[jax.ShapeDtypeStruct(fold_shape, F32)] * 5,
        in_specs=[pl.BlockSpec(memory_space=pl.ANY)] * 10,
        out_specs=[pl.BlockSpec(memory_space=pltpu.VMEM)] * 5,
        scratch_shapes=scratch,
        compiler_params=pltpu.CompilerParams(
            collective_id=0, has_side_effects=True, vmem_limit_bytes=60 * 2**20
        ),
    )(
        pressure_init.reshape(fold_shape),
        gap_height.reshape(fold_shape),
        active.reshape(fold_shape),
        self_compliance.reshape(fold_shape),
        near_blocks,
        near_list,
        far_list,
        source_basis.reshape(CL * RANK, CS),
        target_basis.reshape(CL * RANK, CS),
        jnp.transpose(coupling, (1, 0, 2)),
    )
    pressure = pressure - step * direction
    gap = gap - step * image
    return pressure.reshape(elements), gap.reshape(elements)


def solution(mesh):
    spec = P(("group", "member"))
    return jax.shard_map(
        shards, mesh=mesh, in_specs=(spec,) * 10, out_specs=(spec, spec), check_vma=False
    )
```
